32 devices in a mesh: chaos: 4 (over y, x), space: 8 (over z, core).
Axes of the slice: x: 2, y: 2, z: 4, core: 2. Of those that a mesh axis runs over, the one named last changes fastest.
Arguments:
- modes: float32 [120, 64, 2048], P('chaos', 'space'), may hold values from -2 to 2
- kl_fields: float32 [8, 64, 2048], P(None, 'space'), may hold values from 0.1 to 1
- triples: int32 [624, 3], replicated, may hold values from 0 to 119, as said below
- ratios: int32 [624, 2], replicated, may hold values from 1 to 12, as said below
- mode_of_slot: int32 [120], replicated, may hold values from 0 to 119, each once
Outputs:
- applied: float32 [120, 64, 2048], P('chaos', 'space')
The draws below stay inside these ranges and needn't reach their ends.
Inputs may be any that keep to these rules, and one draw needn't show every extreme that they name: `triples`: rows are distinct. Modes are the multi-indices of total degree at most 3 in 7 variables. Every mode i has the row (i, i, 0); every other row (i, j, k) has k of 1 or more, and the multi-indices of i and j differ by one in variable k and agree elsewhere; each such pair appears in both orders. `ratios`: column 0 is a positive numerator, column 1 a denominator of 1 to 4. `mode_of_slot`: A permutation.
All inputs are finite; a program needn't handle non-finite values.
Results may differ from the reference program's by a relative error of at most 0.000082.
Values sent between devices are 32-bit elements; how exact they have to be, the bound alone decides.
A program may use at most 128 MiB of HBM per device.

```python
import math
import jax
import jax.numpy as jnp
import numpy as np
from jax import lax

KL_TERMS = 8
MODES = 120
COLS = 2048
ROWS = 64


def hermite_table():
    variables = KL_TERMS - 1
    combos = [()]
    for position in range(variables):
        combos = [prefix + (degree,) for prefix in combos for degree in range(4) if sum(prefix) + degree <= 3]
    lookup = {}
    for number, combo in enumerate(combos):
        lookup[combo] = number
    entries = []
    for combo in combos:
        entries.append((lookup[combo], lookup[combo], 0, 1))
    for combo in combos:
        if sum(combo) < 3:
            for position in range(variables):
                raised = combo[:position] + (combo[position] + 1,) + combo[position + 1:]
                lower_mode = lookup[combo]
                upper_mode = lookup[raised]
                entries.append((lower_mode, upper_mode, position + 1, combo[position] + 1))
                entries.append((upper_mode, lower_mode, position + 1, 1))
    return np.array(entries, dtype=np.int32)


def hermite_rows(key):
    table = jnp.asarray(hermite_table())
    shuffle = jax.random.permutation(jax.random.fold_in(key, 7), table.shape[0])
    return table[shuffle]


def draw_triples(key, part):
    return hermite_rows(key)[:, :3].astype(jnp.int32)


def draw_ratios(key, part):
    table_rows = hermite_rows(key)
    split_keys = jax.random.split(jax.random.fold_in(key, 13), 2)
    amplitude = jax.random.randint(split_keys[0], (KL_TERMS,), 1, 5).at[1].set(4).at[0].set(1)
    divisor = jax.random.randint(split_keys[1], (KL_TERMS,), 1, 5).at[2].set(4).at[0].set(1)
    numerator = table_rows[:, 3] * amplitude[table_rows[:, 2]]
    denominator = divisor[table_rows[:, 2]]
    return jnp.stack([numerator, denominator], axis=1).astype(jnp.int32)


def level_of(key, shape, cuts, smallest, largest):
    def one(axis_at, blocks):
        heights = jax.random.uniform(jax.random.fold_in(jax.random.fold_in(key, 6), axis_at), (blocks,), jnp.float32, smallest / len(cuts), largest / len(cuts))
        return jnp.repeat(jnp.exp(heights), shape[axis_at] // blocks).reshape((-1,) + (1,) * (len(shape) - axis_at - 1))

    gain = one(*cuts[0])
    for cut in cuts[1:]:
        gain = gain * one(*cut)
    return gain


def normal_values(rng, dims, width, reach, pieces=(), kind=jnp.bfloat16):
    gain = level_of(rng, dims, pieces, -0.22, 0.18) if pieces else 1.0
    values = jax.random.normal(rng, dims, jnp.float32) * width * gain
    return jnp.minimum(jnp.maximum(values, -reach), reach).astype(kind)


def setup_inputs(seed: int = 0) -> dict:
    key_list = jax.random.split(jax.random.key(seed), 6)
    return {
        "modes": normal_values(key_list[0], (MODES, ROWS, COLS), 0.3, 2.0, ((0, 4), (1, 8)), jnp.float32),
        "kl_fields": jnp.clip(jnp.exp(math.log(1.0) - 2.3025851 * jax.random.uniform(key_list[1], (KL_TERMS, ROWS, COLS), jnp.float32) ** level_of(key_list[1], (KL_TERMS, ROWS, COLS), ((1, 8),), -0.2, 0.2)), 0.1, 1.0),
        "triples": draw_triples(jax.random.fold_in(key_list[5], 71), 0),
        "ratios": draw_ratios(jax.random.fold_in(key_list[5], 71), 0),
        "mode_of_slot": jax.random.permutation(key_list[4], MODES).astype(jnp.int32),
    }


def diffuse(values, factor):
    center = values[:, 1:-1, :]
    coef_mid = factor[1:-1, :]
    result = (coef_mid + factor[:-2, :]) * (center - values[:, :-2, :])
    result = result + (coef_mid + factor[2:, :]) * (center - values[:, 2:, :])
    zero_col = jnp.zeros_like(center[:, :, :1])
    left_cell = jnp.concatenate([zero_col, center[:, :, :-1]], axis=2)
    right_cell = jnp.concatenate([center[:, :, 1:], zero_col], axis=2)
    coef_zero = jnp.zeros_like(coef_mid[:, :1])
    coef_left = jnp.concatenate([coef_zero, coef_mid[:, :-1]], axis=1)
    coef_right = jnp.concatenate([coef_mid[:, 1:], coef_zero], axis=1)
    result = result + (coef_mid + coef_left) * (center - left_cell)
    result = result + (coef_mid + coef_right) * (center - right_cell)
    return 0.5 * result


def reference(modes, kl_fields, triples, ratios, mode_of_slot):
    mode_count = modes.shape[0]
    matches = triples[:, :2, None] == mode_of_slot[None, None, :]
    slot_pairs = jnp.sum(jnp.where(matches, jnp.arange(mode_count, dtype=jnp.int32), 0), axis=2).astype(jnp.int32)
    weights = ratios[:, 0].astype(jnp.float32) / ratios[:, 1].astype(jnp.float32)
    padded_modes = jnp.pad(modes, ((0, 0), (1, 1), (0, 0)))
    padded_coef = jnp.pad(kl_fields, ((0, 0), (1, 1), (0, 0)))

    def accumulate(running, triple_item):
        slot_pair, kl_index, weight = triple_item
        one_field = lax.dynamic_slice_in_dim(padded_modes, slot_pair[1], 1, 0)
        factor = lax.dynamic_slice_in_dim(padded_coef, kl_index, 1, 0)[0]
        stencil_image = weight * diffuse(one_field, factor)
        current = lax.dynamic_slice_in_dim(running, slot_pair[0], 1, 0)
        running = lax.dynamic_update_slice_in_dim(running, current + stencil_image, slot_pair[0], 0)
        return running, None

    running, _ = lax.scan(accumulate, jnp.zeros(modes.shape, jnp.float32), (slot_pairs, triples[:, 2], weights))
    return running
```

```python
import functools

import jax
import jax.numpy as jnp
from jax import lax
from jax.experimental import pallas as pl
from jax.experimental.pallas import tpu as pltpu
from jax.sharding import PartitionSpec as P

MESH = pl.DeviceIdType.MESH
LANES = 128
SCALE = 0.5 / 12.0


def galerkin_kernel(
    groups, slabs, xt, klt, table, slot_col, out,
    field, edges, edge_send, kl_rim, weights, split, done,
    fwd_send, fwd_recv, bwd_send, bwd_recv, own_sem, back_sem,
    edge_ssem, edge_rsem, rim_ssem, rim_rsem, kl_ssem, kl_rsem,
):
    me = lax.axis_index("chaos")
    slab = lax.axis_index("space")
    rows, own, cols = xt.shape
    kl_terms = klt.shape[1]
    total = groups * own
    width = cols // groups
    base = pl.multiple_of(me * width, LANES)
    my_rows = pl.ds(pl.multiple_of(me * own, 8), own)
    has_prev = slab > 0
    has_next = slab < slabs - 1
    partners = [lax.rem(me + off, groups) for off in range(1, groups)]

    barrier = pltpu.get_barrier_semaphore()
    for peer in partners:
        pl.semaphore_signal(barrier, inc=1, device_id={"chaos": peer}, device_id_type=MESH)

    @pl.when(has_prev)
    def _():
        pl.semaphore_signal(barrier, inc=1, device_id={"space": slab - 1}, device_id_type=MESH)

    @pl.when(has_next)
    def _():
        pl.semaphore_signal(barrier, inc=1, device_id={"space": slab + 1}, device_id_type=MESH)

    ends = jnp.where(has_prev, 1, 0) + jnp.where(has_next, 1, 0)
    pl.semaphore_wait(barrier, groups - 1 + ends)

    def forward(r, n):
        peer = partners[n]
        return pltpu.make_async_remote_copy(
            src_ref=xt.at[r, :, pl.ds(pl.multiple_of(peer * width, LANES), width)],
            dst_ref=field.at[r + 1, my_rows],
            send_sem=fwd_send.at[r, n], recv_sem=fwd_recv.at[r, n],
            device_id={"chaos": peer}, device_id_type=MESH,
        )

    def own_copy(r):
        return pltpu.make_async_copy(
            xt.at[r, :, pl.ds(base, width)], field.at[r + 1, my_rows], own_sem.at[r]
        )

    def backward(r, n):
        peer = partners[n]
        return pltpu.make_async_remote_copy(
            src_ref=done.at[r, pl.ds(pl.multiple_of(peer * own, 8), own)],
            dst_ref=out.at[r, :, pl.ds(base, width)],
            send_sem=bwd_send.at[r, n], recv_sem=bwd_recv.at[r, n],
            device_id={"chaos": peer}, device_id_type=MESH,
        )

    def back_copy(r):
        return pltpu.make_async_copy(
            done.at[r, my_rows], out.at[r, :, pl.ds(base, width)], back_sem.at[r]
        )

    def edge_copy(n):
        return pltpu.make_async_remote_copy(
            src_ref=edge_send.at[partners[n]], dst_ref=edges.at[my_rows],
            send_sem=edge_ssem.at[n], recv_sem=edge_rsem.at[n],
            device_id={"chaos": partners[n]}, device_id_type=MESH,
        )

    def rim_copy(up):
        return pltpu.make_async_remote_copy(
            src_ref=field.at[1 if up else rows], dst_ref=field.at[rows + 1 if up else 0],
            send_sem=rim_ssem.at[up], recv_sem=rim_rsem.at[up],
            device_id={"space": slab - 1 if up else slab + 1}, device_id_type=MESH,
        )

    def kl_copy(up):
        return pltpu.make_async_remote_copy(
            src_ref=klt.at[0 if up else rows - 1, :, pl.ds(base, width)],
            dst_ref=kl_rim.at[1 if up else 0],
            send_sem=kl_ssem.at[up], recv_sem=kl_rsem.at[up],
            device_id={"space": slab - 1 if up else slab + 1}, device_id_type=MESH,
        )

    def start_row(r):
        own_copy(r).start()
        for n in range(groups - 1):
            forward(r, n).start()

    def wait_row(r):
        own_copy(r).wait()
        for n in range(groups - 1):
            forward(r, n).wait_recv()

    def send_row(r):
        back_copy(r).start()
        for n in range(groups - 1):
            backward(r, n).start()

    start_row(rows - 1)
    start_row(0)

    @pl.when(has_prev)
    def _():
        kl_copy(1).start()

    @pl.when(has_next)
    def _():
        kl_copy(0).start()

    lane = lax.broadcasted_iota(jnp.int32, (own, LANES), 1)
    cut_left = [jnp.zeros((own, LANES), jnp.float32) for _ in range(groups)]
    for r in range(rows):
        for g in range(groups + 1):
            for side, slot in ((0, r), (1, rows + r)):
                target = g if side == 0 else g - 1
                if target < 0 or target >= groups:
                    continue
                value = jnp.zeros((own, LANES), jnp.float32)
                if g < groups:
                    value = pltpu.roll(xt[r, :, g * width : g * width + LANES], slot, 1)
                if g > 0:
                    value = value - pltpu.roll(xt[r, :, g * width - LANES : g * width], slot + 1, 1)
                cut_left[target] = jnp.where(lane == slot, value, cut_left[target])
    for g in range(groups):
        edge_send[g] = cut_left[g]
    for n in range(groups - 1):
        edge_copy(n).start()

    def start_more(r, carry):
        start_row(r)
        return carry

    lax.fori_loop(1, rows - 1, start_more, 0)
    edges[my_rows, :] = edge_send[me]

    first, second, term = table[0:1, :], table[1:2, :], table[2:3, :]
    over = table[4:5, :]
    twelfths = jnp.where(over == 1, 12, jnp.where(over == 2, 6, jnp.where(over == 3, 4, 3)))
    amount = (table[3:4, :] * twelfths).astype(jnp.float32)
    mode = slot_col[:, 0:1]
    hit_first = jnp.where(mode == first, 1.0, 0.0).astype(jnp.bfloat16)
    hit_second = mode == second
    for k in range(kl_terms):
        picked = jnp.where(hit_second, jnp.where(term == k, amount, 0.0), 0.0).astype(jnp.bfloat16)
        block = lax.dot_general(
            hit_first, picked, (((1,), (1,)), ((), ())), preferred_element_type=jnp.float32
        ).astype(jnp.bfloat16)
        weights[k, :, 0:total] = block
        weights[k, :, total : 2 * total] = block

    def flux(diff, coef):
        size = diff.shape[1]
        high = diff.astype(jnp.bfloat16)
        split[0:total, 0:size] = high
        split[total : 2 * total, 0:size] = (diff - high.astype(jnp.float32)).astype(jnp.bfloat16)
        result = None
        for k in range(kl_terms):
            mixed = jnp.dot(
                weights[k], split[:, 0:size], preferred_element_type=jnp.float32
            )
            part = coef[k : k + 1, :] * mixed
            result = part if result is None else result + part
        return result

    kl_lane = lax.broadcasted_iota(jnp.int32, (kl_terms, LANES), 1)
    before = pl.multiple_of(jnp.maximum(base - LANES, 0), LANES)
    after = pl.multiple_of(lax.rem(base + width, cols), LANES)
    not_first = jnp.where(me > 0, 1.0, 0.0)
    not_last = jnp.where(me < groups - 1, 1.0, 0.0)
    cut_coef = jnp.zeros((kl_terms, LANES), jnp.float32)
    for r in range(rows):
        here = pltpu.roll(klt[r, :, pl.ds(base, LANES)], r, 1) if r else klt[r, :, pl.ds(base, LANES)]
        there = pltpu.roll(klt[r, :, pl.ds(before, LANES)], r + 1, 1)
        cut_coef = jnp.where(kl_lane == r, (here + not_first * there) * SCALE, cut_coef)

    for n in range(groups - 1):
        edge_copy(n).wait_recv()
    total_lane = lax.broadcasted_iota(jnp.int32, (total, LANES), 1)
    cut_diff = edges[...]
    cut_flux = flux(jnp.where(total_lane < rows, cut_diff, 0.0), cut_coef)
    edge_send_flux = cut_flux

    wide_lane = lax.broadcasted_iota(jnp.int32, (total, width), 1)
    coef_lane = lax.broadcasted_iota(jnp.int32, (kl_terms, width), 1)

    def across(r):
        x = field[r + 1]
        right = jnp.sum(jnp.where(total_lane == rows + r, edges[...], 0.0), axis=1, keepdims=True)
        diff = jnp.where(wide_lane == width - 1, right, pltpu.roll(x, width - 1, 1) - x)
        a = klt[r, :, pl.ds(base, width)]
        a_next = klt[r, :, pl.ds(after, LANES)][:, 0:1] * not_last
        coef = (a + jnp.where(coef_lane == width - 1, a_next, pltpu.roll(a, width - 1, 1))) * SCALE
        flow = flux(diff, coef)
        left = jnp.sum(jnp.where(total_lane == r, edge_send_flux, 0.0), axis=1, keepdims=True)
        return jnp.where(wide_lane == 0, left, pltpu.roll(flow, 1, 1)) - flow

    wait_row(rows - 1)
    wait_row(0)

    @pl.when(has_prev)
    def _():
        rim_copy(1).start()

    @pl.when(has_next)
    def _():
        rim_copy(0).start()

    done[0] = across(0)

    def one_row(r, carry):
        @pl.when(r < rows - 1)
        def _():
            wait_row(r)

        coef = (klt[r - 1, :, pl.ds(base, width)] + klt[r, :, pl.ds(base, width)]) * SCALE
        down = flux(field[r + 1] - field[r], coef)
        done[r - 1] = done[r - 1] - down
        done[r] = across(r) + down

        @pl.when(r > 1)
        def _():
            send_row(r - 1)

        return carry

    lax.fori_loop(1, rows, one_row, 0)

    @pl.when(has_prev)
    def _():
        rim_copy(0).wait_recv()
        kl_copy(0).wait_recv()

    @pl.when(jnp.logical_not(has_prev))
    def _():
        field[0] = jnp.zeros((total, width), jnp.float32)
        kl_rim[0] = jnp.zeros((kl_terms, width), jnp.float32)

    @pl.when(has_next)
    def _():
        rim_copy(1).wait_recv()
        kl_copy(1).wait_recv()

    @pl.when(jnp.logical_not(has_next))
    def _():
        field[rows + 1] = jnp.zeros((total, width), jnp.float32)
        kl_rim[1] = jnp.zeros((kl_terms, width), jnp.float32)

    coef = (kl_rim[0] + klt[0, :, pl.ds(base, width)]) * SCALE
    done[0] = done[0] + flux(field[1] - field[0], coef)
    send_row(0)
    coef = (kl_rim[1] + klt[rows - 1, :, pl.ds(base, width)]) * SCALE
    done[rows - 1] = done[rows - 1] - flux(field[rows + 1] - field[rows], coef)
    send_row(rows - 1)

    def finish(r, carry):
        back_copy(r).wait()
        for n in range(groups - 1):
            forward(r, n).wait_send()
            backward(r, n).wait()
        return carry

    lax.fori_loop(0, rows, finish, 0)
    for n in range(groups - 1):
        edge_copy(n).wait_send()

    @pl.when(has_prev)
    def _():
        rim_copy(1).wait_send()
        kl_copy(1).wait_send()

    @pl.when(has_next)
    def _():
        rim_copy(0).wait_send()
        kl_copy(0).wait_send()


def local(modes, kl_fields, triples, ratios, mode_of_slot):
    groups, slabs = lax.axis_size("chaos"), lax.axis_size("space")
    own, rows, cols = modes.shape
    kl_terms = kl_fields.shape[0]
    padded = -(-own // 8) * 8
    total = groups * padded
    width = cols // groups
    xt = jnp.pad(jnp.transpose(modes, (1, 0, 2)), ((0, 0), (0, padded - own), (0, 0)))
    klt = jnp.transpose(kl_fields, (1, 0, 2))
    count = triples.shape[0]
    table = jnp.concatenate([triples, ratios], axis=1).T
    table = jnp.pad(table, ((0, 3), (0, -count % LANES)), constant_values=-1)
    slots = jnp.pad(mode_of_slot.reshape(groups, own), ((0, 0), (0, padded - own)), constant_values=-2)
    slot_col = jnp.broadcast_to(slots.reshape(total, 1), (total, LANES))
    vmem = pl.BlockSpec(memory_space=pltpu.VMEM)
    dma = pltpu.SemaphoreType.DMA
    result = pl.pallas_call(
        functools.partial(galerkin_kernel, groups, slabs),
        out_shape=jax.ShapeDtypeStruct((rows, padded, cols), jnp.float32),
        in_specs=[vmem] * 4,
        out_specs=pl.BlockSpec(memory_space=pl.ANY),
        scratch_shapes=[
            pltpu.VMEM((rows + 2, total, width), jnp.float32),
            pltpu.VMEM((total, LANES), jnp.float32),
            pltpu.VMEM((groups, padded, LANES), jnp.float32),
            pltpu.VMEM((2, kl_terms, width), jnp.float32),
            pltpu.VMEM((kl_terms, total, 2 * total), jnp.bfloat16),
            pltpu.VMEM((2 * total, width), jnp.bfloat16),
            pltpu.VMEM((rows, total, width), jnp.float32),
            dma((rows, groups - 1)), dma((rows, groups - 1)),
            dma((rows, groups - 1)), dma((rows, groups - 1)),
            dma((rows,)), dma((rows,)),
            dma((groups - 1,)), dma((groups - 1,)),
            dma((2,)), dma((2,)), dma((2,)), dma((2,)),
        ],
        compiler_params=pltpu.CompilerParams(
            collective_id=0, has_side_effects=True, vmem_limit_bytes=32 * 1024 * 1024
        ),
    )(xt, klt, table, slot_col)
    return jnp.transpose(result[:, :own], (1, 0, 2))


def solution(mesh):
    return jax.shard_map(
        local,
        mesh=mesh,
        in_specs=(P("chaos", "space", None), P(None, "space", None), P(), P(), P()),
        out_specs=P("chaos", "space", None),
        check_vma=False,
    )
```

```python
import functools

import jax
import jax.numpy as jnp
from jax import lax
from jax.experimental import pallas as pl
from jax.experimental.pallas import tpu as pltpu
from jax.sharding import PartitionSpec as P

MESH = pl.DeviceIdType.MESH
LANES = 128
SCALE = 0.5 / 12.0


def galerkin_kernel(
    groups, slabs, modes, kl, triples, ratios, slots, out,
    xt, klt, field, edges, edge_send, kl_rim, weights, split, done, stage,
    fwd_send, fwd_recv, bwd_send, bwd_recv, own_sem, back_sem,
    edge_ssem, edge_rsem, rim_ssem, rim_rsem, kl_ssem, kl_rsem,
):
    me = lax.axis_index("chaos")
    slab = lax.axis_index("space")
    own, rows, cols = modes.shape
    kl_terms = kl.shape[0]
    room = -(-own // 8) * 8
    total = groups * room
    width = cols // groups
    base = pl.multiple_of(me * width, LANES)
    my_edges = pl.ds(pl.multiple_of(me * room, 8), room)
    has_prev = slab > 0
    has_next = slab < slabs - 1
    partners = [lax.rem(me + off, groups) for off in range(1, groups)]

    barrier = pltpu.get_barrier_semaphore()
    for peer in partners:
        pl.semaphore_signal(barrier, inc=1, device_id={"chaos": peer}, device_id_type=MESH)

    @pl.when(has_prev)
    def _():
        pl.semaphore_signal(barrier, inc=1, device_id={"space": slab - 1}, device_id_type=MESH)

    @pl.when(has_next)
    def _():
        pl.semaphore_signal(barrier, inc=1, device_id={"space": slab + 1}, device_id_type=MESH)

    ends = jnp.where(has_prev, 1, 0) + jnp.where(has_next, 1, 0)
    pl.semaphore_wait(barrier, groups - 1 + ends)

    def forward(r, n):
        peer = partners[n]
        return pltpu.make_async_remote_copy(
            src_ref=xt.at[r, :, pl.ds(pl.multiple_of(peer * width, LANES), width)],
            dst_ref=field.at[r + 1, me],
            send_sem=fwd_send.at[r, n], recv_sem=fwd_recv.at[r, n],
            device_id={"chaos": peer}, device_id_type=MESH,
        )

    def own_copy(r):
        return pltpu.make_async_copy(
            xt.at[r, :, pl.ds(base, width)], field.at[r + 1, me], own_sem.at[r]
        )

    def backward(r, n):
        peer = partners[n]
        return pltpu.make_async_remote_copy(
            src_ref=done.at[r, peer],
            dst_ref=out.at[r, :, pl.ds(base, width)],
            send_sem=bwd_send.at[r, n], recv_sem=bwd_recv.at[r, n],
            device_id={"chaos": peer}, device_id_type=MESH,
        )

    def back_copy(r):
        return pltpu.make_async_copy(
            done.at[r, me], out.at[r, :, pl.ds(base, width)], back_sem.at[r]
        )

    def edge_copy(n):
        return pltpu.make_async_remote_copy(
            src_ref=edge_send.at[partners[n]], dst_ref=edges.at[my_edges],
            send_sem=edge_ssem.at[n], recv_sem=edge_rsem.at[n],
            device_id={"chaos": partners[n]}, device_id_type=MESH,
        )

    def rim_copy(up):
        return pltpu.make_async_remote_copy(
            src_ref=field.at[1 if up else rows], dst_ref=field.at[rows + 1 if up else 0],
            send_sem=rim_ssem.at[up], recv_sem=rim_rsem.at[up],
            device_id={"space": slab - 1 if up else slab + 1}, device_id_type=MESH,
        )

    def kl_copy(up):
        return pltpu.make_async_remote_copy(
            src_ref=klt.at[0 if up else rows - 1, :, pl.ds(base, width)],
            dst_ref=kl_rim.at[1 if up else 0],
            send_sem=kl_ssem.at[up], recv_sem=kl_rsem.at[up],
            device_id={"space": slab - 1 if up else slab + 1}, device_id_type=MESH,
        )

    def start_row(r):
        own_copy(r).start()
        for n in range(groups - 1):
            forward(r, n).start()

    def wait_row(r):
        own_copy(r).wait()
        for n in range(groups - 1):
            forward(r, n).wait_recv()

    def send_row(r):
        back_copy(r).start()
        for n in range(groups - 1):
            backward(r, n).start()

    for r in [rows - 1] + list(range(rows - 1)):
        xt[r] = modes[:, r, :]
        start_row(r)
    for r in [0, rows - 1] + list(range(1, rows - 1)):
        klt[r] = kl[:, r, :]

    @pl.when(has_prev)
    def _():
        kl_copy(1).start()

    @pl.when(has_next)
    def _():
        kl_copy(0).start()

    lane = lax.broadcasted_iota(jnp.int32, (own, LANES), 1)
    cut_left = [jnp.zeros((own, LANES), jnp.float32) for _ in range(groups)]
    for r in range(rows):
        for g in range(groups + 1):
            for side, slot in ((0, r), (1, rows + r)):
                target = g if side == 0 else g - 1
                if target < 0 or target >= groups:
                    continue
                value = jnp.zeros((own, LANES), jnp.float32)
                if g < groups:
                    value = pltpu.roll(xt[r, :, g * width : g * width + LANES], slot, 1)
                if g > 0:
                    value = value - pltpu.roll(xt[r, :, g * width - LANES : g * width], slot + 1, 1)
                cut_left[target] = jnp.where(lane == slot, value, cut_left[target])
    for g in range(groups):
        edge_send[g] = jnp.zeros((room, LANES), jnp.float32)
        edge_send[g, 0:own] = cut_left[g]
    for n in range(groups - 1):
        edge_copy(n).start()

    edges[my_edges, :] = edge_send[me]

    first, second, term = triples[:, 0:1], triples[:, 1:2], triples[:, 2:3]
    over = ratios[:, 1:2]
    twelfths = jnp.where(over == 1, 12, jnp.where(over == 2, 6, jnp.where(over == 3, 4, 3)))
    amount = (ratios[:, 0:1] * twelfths).astype(jnp.float32)
    hit_first = jnp.transpose(jnp.where(slots[...] == first, 1.0, 0.0)).astype(jnp.bfloat16)
    hit_second = jnp.where(slots[...] == second, amount, 0.0)
    for k in range(kl_terms):
        picked = jnp.where(term == k, hit_second, 0.0).astype(jnp.bfloat16)
        block = jnp.dot(hit_first, picked, preferred_element_type=jnp.float32).astype(jnp.bfloat16)
        weights[k, :, 0:total] = block
        weights[k, :, total : 2 * total] = block

    stage[...] = jnp.zeros((total, width), jnp.float32)

    def staged(part):
        for s in range(groups):
            stage[s * room : s * room + own] = part(s)
        return stage[...]

    def store(r, value):
        for s in range(groups):
            done[r, s] = value[s * room : s * room + own]

    def add(r, value):
        for s in range(groups):
            done[r, s] = done[r, s] + value[s * room : s * room + own]

    def flux(diff, coef):
        size = diff.shape[1]
        high = diff.astype(jnp.bfloat16)
        split[0:total, 0:size] = high
        split[total : 2 * total, 0:size] = (diff - high.astype(jnp.float32)).astype(jnp.bfloat16)
        result = None
        for k in range(kl_terms):
            mixed = jnp.dot(
                weights[k], split[:, 0:size], preferred_element_type=jnp.float32
            )
            part = coef[k : k + 1, :] * mixed
            result = part if result is None else result + part
        return result

    kl_lane = lax.broadcasted_iota(jnp.int32, (kl_terms, LANES), 1)
    before = pl.multiple_of(jnp.maximum(base - LANES, 0), LANES)
    after = pl.multiple_of(lax.rem(base + width, cols), LANES)
    not_first = jnp.where(me > 0, 1.0, 0.0)
    not_last = jnp.where(me < groups - 1, 1.0, 0.0)
    cut_coef = jnp.zeros((kl_terms, LANES), jnp.float32)
    for r in range(rows):
        here = pltpu.roll(klt[r, :, pl.ds(base, LANES)], r, 1) if r else klt[r, :, pl.ds(base, LANES)]
        there = pltpu.roll(klt[r, :, pl.ds(before, LANES)], r + 1, 1)
        cut_coef = jnp.where(kl_lane == r, (here + not_first * there) * SCALE, cut_coef)

    for n in range(groups - 1):
        edge_copy(n).wait_recv()
    total_lane = lax.broadcasted_iota(jnp.int32, (total, LANES), 1)
    cut_diff = edges[...]
    cut_flux = flux(jnp.where(total_lane < rows, cut_diff, 0.0), cut_coef)
    edge_send_flux = cut_flux

    wide_lane = lax.broadcasted_iota(jnp.int32, (total, width), 1)
    coef_lane = lax.broadcasted_iota(jnp.int32, (kl_terms, width), 1)

    def across(r):
        x = staged(lambda s: field[r + 1, s])
        right = jnp.sum(jnp.where(total_lane == rows + r, edges[...], 0.0), axis=1, keepdims=True)
        diff = jnp.where(wide_lane == width - 1, right, pltpu.roll(x, width - 1, 1) - x)
        a = klt[r, :, pl.ds(base, width)]
        a_next = klt[r, :, pl.ds(after, LANES)][:, 0:1] * not_last
        coef = (a + jnp.where(coef_lane == width - 1, a_next, pltpu.roll(a, width - 1, 1))) * SCALE
        flow = flux(diff, coef)
        left = jnp.sum(jnp.where(total_lane == r, edge_send_flux, 0.0), axis=1, keepdims=True)
        return jnp.where(wide_lane == 0, left, pltpu.roll(flow, 1, 1)) - flow

    wait_row(rows - 1)
    wait_row(0)

    @pl.when(has_prev)
    def _():
        rim_copy(1).start()

    @pl.when(has_next)
    def _():
        rim_copy(0).start()

    store(0, across(0))

    def one_row(r, carry):
        @pl.when(r < rows - 1)
        def _():
            wait_row(r)

        coef = (klt[r - 1, :, pl.ds(base, width)] + klt[r, :, pl.ds(base, width)]) * SCALE
        down = flux(staged(lambda s: field[r + 1, s] - field[r, s]), coef)
        add(r - 1, -down)
        store(r, across(r) + down)

        @pl.when(r > 1)
        def _():
            send_row(r - 1)

        return carry

    lax.fori_loop(1, rows, one_row, 0)

    @pl.when(has_prev)
    def _():
        rim_copy(0).wait_recv()
        kl_copy(0).wait_recv()

    @pl.when(jnp.logical_not(has_prev))
    def _():
        field[0] = jnp.zeros((groups, own, width), jnp.float32)
        kl_rim[0] = jnp.zeros((kl_terms, width), jnp.float32)

    @pl.when(has_next)
    def _():
        rim_copy(1).wait_recv()
        kl_copy(1).wait_recv()

    @pl.when(jnp.logical_not(has_next))
    def _():
        field[rows + 1] = jnp.zeros((groups, own, width), jnp.float32)
        kl_rim[1] = jnp.zeros((kl_terms, width), jnp.float32)

    coef = (kl_rim[0] + klt[0, :, pl.ds(base, width)]) * SCALE
    add(0, flux(staged(lambda s: field[1, s] - field[0, s]), coef))
    send_row(0)
    coef = (kl_rim[1] + klt[rows - 1, :, pl.ds(base, width)]) * SCALE
    add(rows - 1, -flux(staged(lambda s: field[rows + 1, s] - field[rows, s]), coef))
    send_row(rows - 1)

    def finish(r, carry):
        back_copy(r).wait()
        for n in range(groups - 1):
            forward(r, n).wait_send()
            backward(r, n).wait()
        return carry

    lax.fori_loop(0, rows, finish, 0)
    for n in range(groups - 1):
        edge_copy(n).wait_send()

    @pl.when(has_prev)
    def _():
        rim_copy(1).wait_send()
        kl_copy(1).wait_send()

    @pl.when(has_next)
    def _():
        rim_copy(0).wait_send()
        kl_copy(0).wait_send()


def local(modes, kl_fields, triples, ratios, mode_of_slot):
    groups, slabs = lax.axis_size("chaos"), lax.axis_size("space")
    own, rows, cols = modes.shape
    kl_terms = kl_fields.shape[0]
    padded = -(-own // 8) * 8
    total = groups * padded
    width = cols // groups
    slots = jnp.pad(mode_of_slot.reshape(groups, own), ((0, 0), (0, padded - own)), constant_values=-2)
    slots = slots.reshape(1, total)
    vmem = pl.BlockSpec(memory_space=pltpu.VMEM)
    dma = pltpu.SemaphoreType.DMA
    result = pl.pallas_call(
        functools.partial(galerkin_kernel, groups, slabs),
        out_shape=jax.ShapeDtypeStruct((rows, own, cols), jnp.float32),
        in_specs=[vmem] * 5,
        out_specs=pl.BlockSpec(memory_space=pl.ANY),
        scratch_shapes=[
            pltpu.VMEM((rows, own, cols), jnp.float32),
            pltpu.VMEM((rows, kl_terms, cols), jnp.float32),
            pltpu.VMEM((rows + 2, groups, own, width), jnp.float32),
            pltpu.VMEM((total, LANES), jnp.float32),
            pltpu.VMEM((groups, padded, LANES), jnp.float32),
            pltpu.VMEM((2, kl_terms, width), jnp.float32),
            pltpu.VMEM((kl_terms, total, 2 * total), jnp.bfloat16),
            pltpu.VMEM((2 * total, width), jnp.bfloat16),
            pltpu.VMEM((rows, groups, own, width), jnp.float32),
            pltpu.VMEM((total, width), jnp.float32),
            dma((rows, groups - 1)), dma((rows, groups - 1)),
            dma((rows, groups - 1)), dma((rows, groups - 1)),
            dma((rows,)), dma((rows,)),
            dma((groups - 1,)), dma((groups - 1,)),
            dma((2,)), dma((2,)), dma((2,)), dma((2,)),
        ],
        compiler_params=pltpu.CompilerParams(
            collective_id=0, has_side_effects=True, vmem_limit_bytes=32 * 1024 * 1024
        ),
    )(modes, kl_fields, triples, ratios, slots)
    return jnp.transpose(result, (1, 0, 2))


def solution(mesh):
    return jax.shard_map(
        local,
        mesh=mesh,
        in_specs=(P("chaos", "space", None), P(None, "space", None), P(), P(), P()),
        out_specs=P("chaos", "space", None),
        check_vma=False,
    )
```

```python
import functools

import jax
import jax.numpy as jnp
from jax import lax
from jax.experimental import pallas as pl
from jax.experimental.pallas import tpu as pltpu
from jax.sharding import PartitionSpec as P

MESH = pl.DeviceIdType.MESH
LANES = 128
SCALE = 0.5 / 12.0


def galerkin_kernel(
    groups, slabs, modes, kl, triples, ratios, slots, out,
    xt, klt, field, edges, edge_send, kl_rim, weights, split, done, stage, last_down,
    fwd_send, fwd_recv, bwd_send, bwd_recv, own_sem, back_sem,
    edge_ssem, edge_rsem, rim_ssem, rim_rsem, kl_ssem, kl_rsem,
):
    me = lax.axis_index("chaos")
    slab = lax.axis_index("space")
    own, rows, cols = modes.shape
    kl_terms = kl.shape[0]
    room = -(-own // 8) * 8
    total = groups * room
    width = cols // groups
    base = pl.multiple_of(me * width, LANES)
    my_edges = pl.ds(pl.multiple_of(me * room, 8), room)
    has_prev = slab > 0
    has_next = slab < slabs - 1
    partners = [lax.rem(me + off, groups) for off in range(1, groups)]

    barrier = pltpu.get_barrier_semaphore()
    for peer in partners:
        pl.semaphore_signal(barrier, inc=1, device_id={"chaos": peer}, device_id_type=MESH)

    @pl.when(has_prev)
    def _():
        pl.semaphore_signal(barrier, inc=1, device_id={"space": slab - 1}, device_id_type=MESH)

    @pl.when(has_next)
    def _():
        pl.semaphore_signal(barrier, inc=1, device_id={"space": slab + 1}, device_id_type=MESH)

    ends = jnp.where(has_prev, 1, 0) + jnp.where(has_next, 1, 0)
    pl.semaphore_wait(barrier, groups - 1 + ends)

    def forward(r, n):
        peer = partners[n]
        return pltpu.make_async_remote_copy(
            src_ref=xt.at[r, :, pl.ds(pl.multiple_of(peer * width, LANES), width)],
            dst_ref=field.at[r + 1, me],
            send_sem=fwd_send.at[r, n], recv_sem=fwd_recv.at[r, n],
            device_id={"chaos": peer}, device_id_type=MESH,
        )

    def own_copy(r):
        return pltpu.make_async_copy(
            xt.at[r, :, pl.ds(base, width)], field.at[r + 1, me], own_sem.at[r]
        )

    def backward(r, n):
        peer = partners[n]
        return pltpu.make_async_remote_copy(
            src_ref=done.at[r, peer],
            dst_ref=out.at[r, :, pl.ds(base, width)],
            send_sem=bwd_send.at[r, n], recv_sem=bwd_recv.at[r, n],
            device_id={"chaos": peer}, device_id_type=MESH,
        )

    def back_copy(r):
        return pltpu.make_async_copy(
            done.at[r, me], out.at[r, :, pl.ds(base, width)], back_sem.at[r]
        )

    def edge_copy(n):
        return pltpu.make_async_remote_copy(
            src_ref=edge_send.at[partners[n]], dst_ref=edges.at[my_edges],
            send_sem=edge_ssem.at[n], recv_sem=edge_rsem.at[n],
            device_id={"chaos": partners[n]}, device_id_type=MESH,
        )

    def rim_copy(up):
        return pltpu.make_async_remote_copy(
            src_ref=field.at[1 if up else rows], dst_ref=field.at[rows + 1 if up else 0],
            send_sem=rim_ssem.at[up], recv_sem=rim_rsem.at[up],
            device_id={"space": slab - 1 if up else slab + 1}, device_id_type=MESH,
        )

    def kl_copy(up):
        return pltpu.make_async_remote_copy(
            src_ref=klt.at[0 if up else rows - 1, :, pl.ds(base, width)],
            dst_ref=kl_rim.at[1 if up else 0],
            send_sem=kl_ssem.at[up], recv_sem=kl_rsem.at[up],
            device_id={"space": slab - 1 if up else slab + 1}, device_id_type=MESH,
        )

    def start_row(r):
        own_copy(r).start()
        for n in range(groups - 1):
            forward(r, n).start()

    def wait_row(r):
        own_copy(r).wait()
        for n in range(groups - 1):
            forward(r, n).wait_recv()

    def send_row(r):
        back_copy(r).start()
        for n in range(groups - 1):
            backward(r, n).start()

    for r in [rows - 1] + list(range(rows - 1)):
        xt[r] = modes[:, r, :]
        start_row(r)
    for r in [0, rows - 1] + list(range(1, rows - 1)):
        klt[r] = kl[:, r, :]

    @pl.when(has_prev)
    def _():
        kl_copy(1).start()

    @pl.when(has_next)
    def _():
        kl_copy(0).start()

    lane = lax.broadcasted_iota(jnp.int32, (own, LANES), 1)
    cut_left = [jnp.zeros((own, LANES), jnp.float32) for _ in range(groups)]
    for r in range(rows):
        for g in range(groups + 1):
            for side, slot in ((0, r), (1, rows + r)):
                target = g if side == 0 else g - 1
                if target < 0 or target >= groups:
                    continue
                value = jnp.zeros((own, LANES), jnp.float32)
                if g < groups:
                    value = pltpu.roll(xt[r, :, g * width : g * width + LANES], slot, 1)
                if g > 0:
                    value = value - pltpu.roll(xt[r, :, g * width - LANES : g * width], slot + 1, 1)
                cut_left[target] = jnp.where(lane == slot, value, cut_left[target])
    for g in range(groups):
        edge_send[g] = jnp.zeros((room, LANES), jnp.float32)
        edge_send[g, 0:own] = cut_left[g]
    for n in range(groups - 1):
        edge_copy(n).start()

    edges[my_edges, :] = edge_send[me]

    first, second, term = triples[0:1, :], triples[1:2, :], triples[2:3, :]
    over = ratios[1:2, :]
    twelfths = jnp.where(over == 1, 12, jnp.where(over == 2, 6, jnp.where(over == 3, 4, 3)))
    amount = (ratios[0:1, :] * twelfths).astype(jnp.float32)
    at = lax.broadcasted_iota(jnp.int32, (8, total), 1)
    ids = slots[...].astype(jnp.float32)
    if total > groups * own:
        ids = jnp.concatenate([ids, jnp.zeros((8, total - groups * own), jnp.float32)], axis=1)
    spread = jnp.full((8, total), -2.0, jnp.float32)
    for s in range(groups):
        moved = pltpu.roll(ids, s * (room - own), 1) if s * (room - own) else ids
        spread = jnp.where((at >= s * room) & (at < s * room + own), moved, spread)
    mode = jnp.transpose(jnp.broadcast_to(spread[0:1, :], (total, total)))[:, 0:1].astype(jnp.int32)
    hit_first = jnp.where(mode == first, 1.0, 0.0).astype(jnp.bfloat16)
    hit_second = jnp.where(mode == second, amount, 0.0)
    for k in range(kl_terms):
        picked = jnp.where(term == k, hit_second, 0.0).astype(jnp.bfloat16)
        block = lax.dot_general(
            hit_first, picked, (((1,), (1,)), ((), ())), preferred_element_type=jnp.float32
        ).astype(jnp.bfloat16)
        weights[k * total : (k + 1) * total, 0:total] = block
        weights[k * total : (k + 1) * total, total : 2 * total] = block

    stage[...] = jnp.zeros((total, width), jnp.float32)

    def staged(part):
        for s in range(groups):
            stage[s * room : s * room + own] = part(s)
        return stage[...]

    def store(r, value):
        for s in range(groups):
            done[r, s] = value[s * room : s * room + own]

    def add(r, value):
        for s in range(groups):
            done[r, s] = done[r, s] + value[s * room : s * room + own]

    def flux(diff, coef):
        size = diff.shape[1]
        high = diff.astype(jnp.bfloat16)
        split[0:total, 0:size] = high
        split[total : 2 * total, 0:size] = (diff - high.astype(jnp.float32)).astype(jnp.bfloat16)
        mixed = jnp.dot(weights[...], split[:, 0:size], preferred_element_type=jnp.float32)
        result = coef[0:1, :] * mixed[0:total]
        for k in range(1, kl_terms):
            result = result + coef[k : k + 1, :] * mixed[k * total : (k + 1) * total]
        return result

    kl_lane = lax.broadcasted_iota(jnp.int32, (kl_terms, LANES), 1)
    before = pl.multiple_of(jnp.maximum(base - LANES, 0), LANES)
    after = pl.multiple_of(lax.rem(base + width, cols), LANES)
    not_first = jnp.where(me > 0, 1.0, 0.0)
    not_last = jnp.where(me < groups - 1, 1.0, 0.0)
    cut_coef = jnp.zeros((kl_terms, LANES), jnp.float32)
    for r in range(rows):
        here = pltpu.roll(klt[r, :, pl.ds(base, LANES)], r, 1) if r else klt[r, :, pl.ds(base, LANES)]
        there = pltpu.roll(klt[r, :, pl.ds(before, LANES)], r + 1, 1)
        cut_coef = jnp.where(kl_lane == r, (here + not_first * there) * SCALE, cut_coef)

    for n in range(groups - 1):
        edge_copy(n).wait_recv()
    total_lane = lax.broadcasted_iota(jnp.int32, (total, LANES), 1)
    cut_diff = edges[...]
    cut_flux = flux(jnp.where(total_lane < rows, cut_diff, 0.0), cut_coef)
    edge_send_flux = cut_flux

    wide_lane = lax.broadcasted_iota(jnp.int32, (total, width), 1)
    coef_lane = lax.broadcasted_iota(jnp.int32, (kl_terms, width), 1)

    def across(r):
        x = staged(lambda s: field[r + 1, s])
        right = jnp.sum(jnp.where(total_lane == rows + r, edges[...], 0.0), axis=1, keepdims=True)
        diff = jnp.where(wide_lane == width - 1, right, pltpu.roll(x, width - 1, 1) - x)
        a = klt[r, :, pl.ds(base, width)]
        a_next = klt[r, :, pl.ds(after, LANES)][:, 0:1] * not_last
        coef = (a + jnp.where(coef_lane == width - 1, a_next, pltpu.roll(a, width - 1, 1))) * SCALE
        flow = flux(diff, coef)
        left = jnp.sum(jnp.where(total_lane == r, edge_send_flux, 0.0), axis=1, keepdims=True)
        return jnp.where(wide_lane == 0, left, pltpu.roll(flow, 1, 1)) - flow

    wait_row(rows - 1)
    wait_row(0)

    @pl.when(has_prev)
    def _():
        rim_copy(1).start()

    @pl.when(has_next)
    def _():
        rim_copy(0).start()

    store(0, across(0))

    def one_row(r, carry):
        @pl.when(r < rows - 1)
        def _():
            wait_row(r)

        coef = (klt[r - 1, :, pl.ds(base, width)] + klt[r, :, pl.ds(base, width)]) * SCALE
        down = flux(staged(lambda s: field[r + 1, s] - field[r, s]), coef)
        add(r - 1, -down)

        @pl.when(r > 1)
        def _():
            send_row(r - 1)

        store(r, across(r) + down)
        return carry

    half = rows // 2
    lax.fori_loop(1, half, one_row, 0)

    @pl.when(has_prev)
    def _():
        rim_copy(0).wait_recv()
        kl_copy(0).wait_recv()

    @pl.when(jnp.logical_not(has_prev))
    def _():
        field[0] = jnp.zeros((groups, own, width), jnp.float32)
        kl_rim[0] = jnp.zeros((kl_terms, width), jnp.float32)

    @pl.when(has_next)
    def _():
        rim_copy(1).wait_recv()
        kl_copy(1).wait_recv()

    @pl.when(jnp.logical_not(has_next))
    def _():
        field[rows + 1] = jnp.zeros((groups, own, width), jnp.float32)
        kl_rim[1] = jnp.zeros((kl_terms, width), jnp.float32)

    coef = (kl_rim[0] + klt[0, :, pl.ds(base, width)]) * SCALE
    add(0, flux(staged(lambda s: field[1, s] - field[0, s]), coef))
    send_row(0)
    coef = (kl_rim[1] + klt[rows - 1, :, pl.ds(base, width)]) * SCALE
    last = flux(staged(lambda s: field[rows + 1, s] - field[rows, s]), coef)
    for s in range(groups):
        last_down[s] = last[s * room : s * room + own]
    lax.fori_loop(half, rows, one_row, 0)
    for s in range(groups):
        done[rows - 1, s] = done[rows - 1, s] - last_down[s]
    send_row(rows - 1)

    def finish(r, carry):
        back_copy(r).wait()
        for n in range(groups - 1):
            forward(r, n).wait_send()
            backward(r, n).wait()
        return carry

    lax.fori_loop(0, rows, finish, 0)
    for n in range(groups - 1):
        edge_copy(n).wait_send()

    @pl.when(has_prev)
    def _():
        rim_copy(1).wait_send()
        kl_copy(1).wait_send()

    @pl.when(has_next)
    def _():
        rim_copy(0).wait_send()
        kl_copy(0).wait_send()


def local(modes, kl_fields, triples, ratios, mode_of_slot):
    groups, slabs = lax.axis_size("chaos"), lax.axis_size("space")
    own, rows, cols = modes.shape
    kl_terms = kl_fields.shape[0]
    padded = -(-own // 8) * 8
    total = groups * padded
    width = cols // groups
    slots = jnp.broadcast_to(mode_of_slot, (8, mode_of_slot.shape[0]))
    vmem = pl.BlockSpec(memory_space=pltpu.VMEM)
    dma = pltpu.SemaphoreType.DMA
    result = pl.pallas_call(
        functools.partial(galerkin_kernel, groups, slabs),
        out_shape=jax.ShapeDtypeStruct((rows, own, cols), jnp.float32),
        in_specs=[vmem] * 5,
        out_specs=pl.BlockSpec(memory_space=pl.ANY),
        scratch_shapes=[
            pltpu.VMEM((rows, own, cols), jnp.float32),
            pltpu.VMEM((rows, kl_terms, cols), jnp.float32),
            pltpu.VMEM((rows + 2, groups, own, width), jnp.float32),
            pltpu.VMEM((total, LANES), jnp.float32),
            pltpu.VMEM((groups, padded, LANES), jnp.float32),
            pltpu.VMEM((2, kl_terms, width), jnp.float32),
            pltpu.VMEM((kl_terms * total, 2 * total), jnp.bfloat16),
            pltpu.VMEM((2 * total, width), jnp.bfloat16),
            pltpu.VMEM((rows, groups, own, width), jnp.float32),
            pltpu.VMEM((total, width), jnp.float32),
            pltpu.VMEM((groups, own, width), jnp.float32),
            dma((rows, groups - 1)), dma((rows, groups - 1)),
            dma((rows, groups - 1)), dma((rows, groups - 1)),
            dma((rows,)), dma((rows,)),
            dma((groups - 1,)), dma((groups - 1,)),
            dma((2,)), dma((2,)), dma((2,)), dma((2,)),
        ],
        compiler_params=pltpu.CompilerParams(
            collective_id=0, has_side_effects=True, vmem_limit_bytes=32 * 1024 * 1024
        ),
    )(modes, kl_fields, triples.T, ratios.T, slots)
    return jnp.transpose(result, (1, 0, 2))


def solution(mesh):
    return jax.shard_map(
        local,
        mesh=mesh,
        in_specs=(P("chaos", "space", None), P(None, "space", None), P(), P(), P()),
        out_specs=P("chaos", "space", None),
        check_vma=False,
    )
```

```python
import functools

import jax
import jax.numpy as jnp
from jax import lax
from jax.experimental import pallas as pl
from jax.experimental.pallas import tpu as pltpu
from jax.sharding import PartitionSpec as P

MESH = pl.DeviceIdType.MESH
LANES = 128
SCALE = 0.5 / 12.0


def galerkin_kernel(
    groups, slabs, modes_hbm, kl_hbm, triples_hbm, ratios_hbm, slots_hbm, out,
    modes, kl, triples, ratios, slots, packed, klt, field, edges, edge_send, kl_rim, weights, split, done, back, stage, last_down,
    fwd_send, fwd_recv, bwd_send, bwd_recv, own_sem, back_sem,
    edge_ssem, edge_rsem, rim_ssem, rim_rsem, kl_ssem, kl_rsem, load_sem,
):
    loads = [
        pltpu.make_async_copy(source, target, load_sem.at[n])
        for n, (source, target) in enumerate((
            (modes_hbm, modes), (kl_hbm, kl), (triples_hbm, triples),
            (ratios_hbm, ratios), (slots_hbm, slots),
        ))
    ]
    for load in loads:
        load.start()
    me = lax.axis_index("chaos")
    slab = lax.axis_index("space")
    own, rows, cols = modes.shape
    kl_terms = kl.shape[0]
    room = -(-own // 8) * 8
    total = groups * room
    width = cols // groups
    base = pl.multiple_of(me * width, LANES)
    tiles = [(t, slice(t * own, (t + 1) * own), slice(t * LANES, (t + 1) * LANES)) for t in range(width // LANES)]
    my_edges = pl.ds(pl.multiple_of(me * room, 8), room)
    has_prev = slab > 0
    has_next = slab < slabs - 1
    partners = [lax.rem(me + off, groups) for off in range(1, groups)]

    barrier = pltpu.get_barrier_semaphore()
    for peer in partners:
        pl.semaphore_signal(barrier, inc=1, device_id={"chaos": peer}, device_id_type=MESH)

    @pl.when(has_prev)
    def _():
        pl.semaphore_signal(barrier, inc=1, device_id={"space": slab - 1}, device_id_type=MESH)

    @pl.when(has_next)
    def _():
        pl.semaphore_signal(barrier, inc=1, device_id={"space": slab + 1}, device_id_type=MESH)

    ends = jnp.where(has_prev, 1, 0) + jnp.where(has_next, 1, 0)
    pl.semaphore_wait(barrier, groups - 1 + ends)

    def forward(r, n):
        peer = partners[n]
        return pltpu.make_async_remote_copy(
            src_ref=packed.at[r, peer],
            dst_ref=field.at[r + 1, me],
            send_sem=fwd_send.at[r, n], recv_sem=fwd_recv.at[r, n],
            device_id={"chaos": peer}, device_id_type=MESH,
        )

    def own_copy(r):
        return pltpu.make_async_copy(
            packed.at[r, me], field.at[r + 1, me], own_sem.at[r]
        )

    def backward(r, n):
        peer = partners[n]
        return pltpu.make_async_remote_copy(
            src_ref=done.at[r, peer],
            dst_ref=back.at[r, me],
            send_sem=bwd_send.at[r, n], recv_sem=bwd_recv.at[r, n],
            device_id={"chaos": peer}, device_id_type=MESH,
        )

    def back_copy(r):
        return pltpu.make_async_copy(
            done.at[r, me], back.at[r, me], back_sem.at[r]
        )

    def edge_copy(n):
        return pltpu.make_async_remote_copy(
            src_ref=edge_send.at[partners[n]], dst_ref=edges.at[my_edges],
            send_sem=edge_ssem.at[n], recv_sem=edge_rsem.at[n],
            device_id={"chaos": partners[n]}, device_id_type=MESH,
        )

    def rim_copy(up):
        return pltpu.make_async_remote_copy(
            src_ref=field.at[1 if up else rows], dst_ref=field.at[rows + 1 if up else 0],
            send_sem=rim_ssem.at[up], recv_sem=rim_rsem.at[up],
            device_id={"space": slab - 1 if up else slab + 1}, device_id_type=MESH,
        )

    def kl_copy(up):
        return pltpu.make_async_remote_copy(
            src_ref=klt.at[0 if up else rows - 1, :, pl.ds(base, width)],
            dst_ref=kl_rim.at[1 if up else 0],
            send_sem=kl_ssem.at[up], recv_sem=kl_rsem.at[up],
            device_id={"space": slab - 1 if up else slab + 1}, device_id_type=MESH,
        )

    def start_row(r):
        own_copy(r).start()
        for n in range(groups - 1):
            forward(r, n).start()

    def wait_row(r):
        own_copy(r).wait()
        for n in range(groups - 1):
            forward(r, n).wait_recv()

    def send_row(r):
        back_copy(r).start()
        for n in range(groups - 1):
            backward(r, n).start()

    loads[0].wait()
    for r in [rows - 1] + list(range(rows - 1)):
        for g in range(groups):
            for t, part, _ in tiles:
                at = g * width + t * LANES
                packed[r, g, part] = modes[:, r, at : at + LANES]
        start_row(r)
    loads[1].wait()
    for r in [0, rows - 1] + list(range(1, rows - 1)):
        klt[r] = kl[:, r, :]

    @pl.when(has_prev)
    def _():
        kl_copy(1).start()

    @pl.when(has_next)
    def _():
        kl_copy(0).start()

    lane = lax.broadcasted_iota(jnp.int32, (own, LANES), 1)
    cut_left = [jnp.zeros((own, LANES), jnp.float32) for _ in range(groups)]
    for r in range(rows):
        for g in range(groups + 1):
            for side, slot in ((0, r), (1, rows + r)):
                target = g if side == 0 else g - 1
                if target < 0 or target >= groups:
                    continue
                value = jnp.zeros((own, LANES), jnp.float32)
                if g < groups:
                    value = pltpu.roll(packed[r, g, tiles[0][1]], slot, 1)
                if g > 0:
                    value = value - pltpu.roll(packed[r, g - 1, tiles[-1][1]], slot + 1, 1)
                cut_left[target] = jnp.where(lane == slot, value, cut_left[target])
    for g in range(groups):
        edge_send[g] = jnp.zeros((room, LANES), jnp.float32)
        edge_send[g, 0:own] = cut_left[g]
    for n in range(groups - 1):
        edge_copy(n).start()

    edges[my_edges, :] = edge_send[me]

    for load in loads[2:]:
        load.wait()
    first, second, term = triples[0:1, :], triples[1:2, :], triples[2:3, :]
    over = ratios[1:2, :]
    twelfths = jnp.where(over == 1, 12, jnp.where(over == 2, 6, jnp.where(over == 3, 4, 3)))
    amount = (ratios[0:1, :] * twelfths).astype(jnp.float32)
    at = lax.broadcasted_iota(jnp.int32, (8, total), 1)
    ids = jnp.broadcast_to(slots[...], (8, groups * own)).astype(jnp.float32)
    if total > groups * own:
        ids = jnp.concatenate([ids, jnp.zeros((8, total - groups * own), jnp.float32)], axis=1)
    spread = jnp.full((8, total), -2.0, jnp.float32)
    for s in range(groups):
        moved = pltpu.roll(ids, s * (room - own), 1) if s * (room - own) else ids
        spread = jnp.where((at >= s * room) & (at < s * room + own), moved, spread)
    mode = jnp.transpose(jnp.broadcast_to(spread[0:1, :], (total, total)))[:, 0:1].astype(jnp.int32)
    hit_first = jnp.where(mode == first, 1.0, 0.0).astype(jnp.bfloat16)
    hit_second = jnp.where(mode == second, amount, 0.0)
    for k in range(kl_terms):
        picked = jnp.where(term == k, hit_second, 0.0).astype(jnp.bfloat16)
        block = lax.dot_general(
            hit_first, picked, (((1,), (1,)), ((), ())), preferred_element_type=jnp.float32
        ).astype(jnp.bfloat16)
        weights[k * total : (k + 1) * total, 0:total] = block
        weights[k * total : (k + 1) * total, total : 2 * total] = block

    stage[...] = jnp.zeros((total, width), jnp.float32)

    def staged(part):
        for s in range(groups):
            for _, rows_of, cols_of in tiles:
                stage[s * room : s * room + own, cols_of] = part(s, rows_of)
        return stage[...]

    def store(target, value):
        for s in range(groups):
            for _, rows_of, cols_of in tiles:
                target[s, rows_of] = value[s * room : s * room + own, cols_of]

    def add(r, value):
        for s in range(groups):
            for _, rows_of, cols_of in tiles:
                done[r, s, rows_of] = done[r, s, rows_of] + value[s * room : s * room + own, cols_of]

    def flux(diff, coef):
        size = diff.shape[1]
        high = diff.astype(jnp.bfloat16)
        split[0:total, 0:size] = high
        split[total : 2 * total, 0:size] = (diff - high.astype(jnp.float32)).astype(jnp.bfloat16)
        mixed = jnp.dot(weights[...], split[:, 0:size], preferred_element_type=jnp.float32)
        result = coef[0:1, :] * mixed[0:total]
        for k in range(1, kl_terms):
            result = result + coef[k : k + 1, :] * mixed[k * total : (k + 1) * total]
        return result

    kl_lane = lax.broadcasted_iota(jnp.int32, (kl_terms, LANES), 1)
    before = pl.multiple_of(jnp.maximum(base - LANES, 0), LANES)
    after = pl.multiple_of(lax.rem(base + width, cols), LANES)
    not_first = jnp.where(me > 0, 1.0, 0.0)
    not_last = jnp.where(me < groups - 1, 1.0, 0.0)
    cut_coef = jnp.zeros((kl_terms, LANES), jnp.float32)
    for r in range(rows):
        here = pltpu.roll(klt[r, :, pl.ds(base, LANES)], r, 1) if r else klt[r, :, pl.ds(base, LANES)]
        there = pltpu.roll(klt[r, :, pl.ds(before, LANES)], r + 1, 1)
        cut_coef = jnp.where(kl_lane == r, (here + not_first * there) * SCALE, cut_coef)

    for n in range(groups - 1):
        edge_copy(n).wait_recv()
    total_lane = lax.broadcasted_iota(jnp.int32, (total, LANES), 1)
    cut_diff = edges[...]
    cut_flux = flux(jnp.where(total_lane < rows, cut_diff, 0.0), cut_coef)
    edge_send_flux = cut_flux

    wide_lane = lax.broadcasted_iota(jnp.int32, (total, width), 1)
    coef_lane = lax.broadcasted_iota(jnp.int32, (kl_terms, width), 1)

    def across(r):
        x = staged(lambda s, p: field[r + 1, s, p])
        right = jnp.sum(jnp.where(total_lane == rows + r, edges[...], 0.0), axis=1, keepdims=True)
        diff = jnp.where(wide_lane == width - 1, right, pltpu.roll(x, width - 1, 1) - x)
        a = klt[r, :, pl.ds(base, width)]
        a_next = klt[r, :, pl.ds(after, LANES)][:, 0:1] * not_last
        coef = (a + jnp.where(coef_lane == width - 1, a_next, pltpu.roll(a, width - 1, 1))) * SCALE
        flow = flux(diff, coef)
        left = jnp.sum(jnp.where(total_lane == r, edge_send_flux, 0.0), axis=1, keepdims=True)
        return jnp.where(wide_lane == 0, left, pltpu.roll(flow, 1, 1)) - flow

    wait_row(rows - 1)
    wait_row(0)

    @pl.when(has_prev)
    def _():
        rim_copy(1).start()

    @pl.when(has_next)
    def _():
        rim_copy(0).start()

    store(done.at[0], across(0))

    def one_row(r, carry):
        @pl.when(r < rows - 1)
        def _():
            wait_row(r)

        coef = (klt[r - 1, :, pl.ds(base, width)] + klt[r, :, pl.ds(base, width)]) * SCALE
        down = flux(staged(lambda s, p: field[r + 1, s, p] - field[r, s, p]), coef)
        add(r - 1, -down)

        @pl.when(r > 1)
        def _():
            send_row(r - 1)

        store(done.at[r], across(r) + down)
        return carry

    half = rows // 2
    lax.fori_loop(1, half, one_row, 0)

    @pl.when(has_prev)
    def _():
        rim_copy(0).wait_recv()
        kl_copy(0).wait_recv()

    @pl.when(jnp.logical_not(has_prev))
    def _():
        field[0] = jnp.zeros(field.shape[1:], jnp.float32)
        kl_rim[0] = jnp.zeros((kl_terms, width), jnp.float32)

    @pl.when(has_next)
    def _():
        rim_copy(1).wait_recv()
        kl_copy(1).wait_recv()

    @pl.when(jnp.logical_not(has_next))
    def _():
        field[rows + 1] = jnp.zeros(field.shape[1:], jnp.float32)
        kl_rim[1] = jnp.zeros((kl_terms, width), jnp.float32)

    coef = (kl_rim[0] + klt[0, :, pl.ds(base, width)]) * SCALE
    add(0, flux(staged(lambda s, p: field[1, s, p] - field[0, s, p]), coef))
    send_row(0)
    coef = (kl_rim[1] + klt[rows - 1, :, pl.ds(base, width)]) * SCALE
    last = flux(staged(lambda s, p: field[rows + 1, s, p] - field[rows, s, p]), coef)
    store(last_down, last)
    lax.fori_loop(half, rows, one_row, 0)
    done[rows - 1] = done[rows - 1] - last_down[...]
    send_row(rows - 1)

    order = list(range(1, half - 1)) + [0] + list(range(half - 1, rows))
    for r in order:
        back_copy(r).wait()
        for n in range(groups - 1):
            backward(r, n).wait_recv()
        for g in range(groups):
            for t, rows_of, _ in tiles:
                at = g * width + t * LANES
                out[:, r, at : at + LANES] = back[r, g, rows_of]

    def finish(r, carry):
        for n in range(groups - 1):
            forward(r, n).wait_send()
            backward(r, n).wait_send()
        return carry

    lax.fori_loop(0, rows, finish, 0)
    for n in range(groups - 1):
        edge_copy(n).wait_send()

    @pl.when(has_prev)
    def _():
        rim_copy(1).wait_send()
        kl_copy(1).wait_send()

    @pl.when(has_next)
    def _():
        rim_copy(0).wait_send()
        kl_copy(0).wait_send()


def local(modes, kl_fields, triples, ratios, mode_of_slot):
    groups, slabs = lax.axis_size("chaos"), lax.axis_size("space")
    own, rows, cols = modes.shape
    kl_terms = kl_fields.shape[0]
    padded = -(-own // 8) * 8
    total = groups * padded
    width = cols // groups
    slots = mode_of_slot.reshape(1, groups * own)
    table, amounts = triples.T, ratios.T
    block = (groups, own * (width // LANES), LANES)
    vmem, dma = pltpu.VMEM, pltpu.SemaphoreType.DMA
    result = pl.pallas_call(
        functools.partial(galerkin_kernel, groups, slabs),
        out_shape=jax.ShapeDtypeStruct((own, rows, cols), jnp.float32),
        in_specs=[pl.BlockSpec(memory_space=pltpu.HBM)] * 5,
        out_specs=pl.BlockSpec(memory_space=pltpu.VMEM),
        scratch_shapes=[
            vmem(modes.shape, jnp.float32),
            vmem(kl_fields.shape, jnp.float32),
            vmem(table.shape, jnp.int32),
            vmem(amounts.shape, jnp.int32),
            vmem(slots.shape, jnp.int32),
            vmem((rows,) + block, jnp.float32),
            vmem((rows, kl_terms, cols), jnp.float32),
            vmem((rows + 2,) + block, jnp.float32),
            vmem((total, LANES), jnp.float32),
            vmem((groups, padded, LANES), jnp.float32),
            vmem((2, kl_terms, width), jnp.float32),
            vmem((kl_terms * total, 2 * total), jnp.bfloat16),
            vmem((2 * total, width), jnp.bfloat16),
            vmem((rows,) + block, jnp.float32),
            vmem((rows,) + block, jnp.float32),
            vmem((total, width), jnp.float32),
            vmem(block, jnp.float32),
            dma((rows, groups - 1)), dma((rows, groups - 1)),
            dma((rows, groups - 1)), dma((rows, groups - 1)),
            dma((rows,)), dma((rows,)),
            dma((groups - 1,)), dma((groups - 1,)),
            dma((2,)), dma((2,)), dma((2,)), dma((2,)), dma((5,)),
        ],
        compiler_params=pltpu.CompilerParams(
            collective_id=0, has_side_effects=True, vmem_limit_bytes=60 * 1024 * 1024
        ),
    )(modes, kl_fields, table, amounts, slots)
    return result


def solution(mesh):
    return jax.shard_map(
        local,
        mesh=mesh,
        in_specs=(P("chaos", "space", None), P(None, "space", None), P(), P(), P()),
        out_specs=P("chaos", "space", None),
        check_vma=False,
    )
```

```python
import functools

import jax
import jax.numpy as jnp
from jax import lax
from jax.experimental import pallas as pl
from jax.experimental.pallas import tpu as pltpu
from jax.sharding import PartitionSpec as P

MESH = pl.DeviceIdType.MESH
LANES = 128
SCALE = 0.5 / 12.0


def galerkin_kernel(
    groups, slabs, modes_hbm, kl_hbm, triples_hbm, ratios_hbm, slots_hbm, out,
    modes, kl, triples, ratios, slots, packed, klt, field, edges, edge_send, kl_rim, weights, split, done, back, stage, last_down,
    fwd_send, fwd_recv, bwd_send, bwd_recv, own_sem, back_sem,
    edge_ssem, edge_rsem, rim_ssem, rim_rsem, kl_ssem, kl_rsem, load_sem,
):
    loads = [
        pltpu.make_async_copy(source, target, load_sem.at[n])
        for n, (source, target) in enumerate((
            (modes_hbm, modes), (kl_hbm, kl), (triples_hbm, triples),
            (ratios_hbm, ratios), (slots_hbm, slots),
        ))
    ]
    for load in loads:
        load.start()
    me = lax.axis_index("chaos")
    slab = lax.axis_index("space")
    own, rows, cols = modes.shape
    kl_terms = kl.shape[0]
    room = -(-own // 8) * 8
    total = groups * room
    width = cols // groups
    base = pl.multiple_of(me * width, LANES)
    tiles = [(t, slice(t * own, (t + 1) * own), slice(t * LANES, (t + 1) * LANES)) for t in range(width // LANES)]
    my_edges = pl.ds(pl.multiple_of(me * room, 8), room)
    has_prev = slab > 0
    has_next = slab < slabs - 1
    partners = [lax.rem(me + off, groups) for off in range(1, groups)]

    barrier = pltpu.get_barrier_semaphore()
    for peer in partners:
        pl.semaphore_signal(barrier, inc=1, device_id={"chaos": peer}, device_id_type=MESH)

    @pl.when(has_prev)
    def _():
        pl.semaphore_signal(barrier, inc=1, device_id={"space": slab - 1}, device_id_type=MESH)

    @pl.when(has_next)
    def _():
        pl.semaphore_signal(barrier, inc=1, device_id={"space": slab + 1}, device_id_type=MESH)

    ends = jnp.where(has_prev, 1, 0) + jnp.where(has_next, 1, 0)
    pl.semaphore_wait(barrier, groups - 1 + ends)

    def forward(r, n):
        peer = partners[n]
        return pltpu.make_async_remote_copy(
            src_ref=packed.at[r, peer],
            dst_ref=field.at[r + 1, me],
            send_sem=fwd_send.at[r, n], recv_sem=fwd_recv.at[r, n],
            device_id={"chaos": peer}, device_id_type=MESH,
        )

    def own_copy(r):
        return pltpu.make_async_copy(
            packed.at[r, me], field.at[r + 1, me], own_sem.at[r]
        )

    def backward(r, n):
        peer = partners[n]
        return pltpu.make_async_remote_copy(
            src_ref=done.at[r, peer],
            dst_ref=back.at[r, me],
            send_sem=bwd_send.at[r, n], recv_sem=bwd_recv.at[r, n],
            device_id={"chaos": peer}, device_id_type=MESH,
        )

    def back_copy(r):
        return pltpu.make_async_copy(
            done.at[r, me], back.at[r, me], back_sem.at[r]
        )

    def edge_copy(n):
        return pltpu.make_async_remote_copy(
            src_ref=edge_send.at[partners[n]], dst_ref=edges.at[my_edges],
            send_sem=edge_ssem.at[n], recv_sem=edge_rsem.at[n],
            device_id={"chaos": partners[n]}, device_id_type=MESH,
        )

    def rim_copy(up):
        return pltpu.make_async_remote_copy(
            src_ref=field.at[1 if up else rows], dst_ref=field.at[rows + 1 if up else 0],
            send_sem=rim_ssem.at[up], recv_sem=rim_rsem.at[up],
            device_id={"space": slab - 1 if up else slab + 1}, device_id_type=MESH,
        )

    def kl_copy(up):
        return pltpu.make_async_remote_copy(
            src_ref=klt.at[0 if up else rows - 1, :, pl.ds(base, width)],
            dst_ref=kl_rim.at[1 if up else 0],
            send_sem=kl_ssem.at[up], recv_sem=kl_rsem.at[up],
            device_id={"space": slab - 1 if up else slab + 1}, device_id_type=MESH,
        )

    def start_row(r):
        own_copy(r).start()
        for n in range(groups - 1):
            forward(r, n).start()

    def wait_row(r):
        own_copy(r).wait()
        for n in range(groups - 1):
            forward(r, n).wait_recv()

    def send_row(r):
        back_copy(r).start()
        for n in range(groups - 1):
            backward(r, n).start()

    loads[0].wait()
    for r in [rows - 1] + list(range(rows - 1)):
        for g in range(groups):
            for t, part, _ in tiles:
                at = g * width + t * LANES
                packed[r, g, part] = modes[:, r, at : at + LANES]
        if r in (rows - 1, 0, 1):
            start_row(r)
    loads[1].wait()
    for r in [0, rows - 1] + list(range(1, rows - 1)):
        klt[r] = kl[:, r, :]

    @pl.when(has_prev)
    def _():
        kl_copy(1).start()

    @pl.when(has_next)
    def _():
        kl_copy(0).start()

    lane = lax.broadcasted_iota(jnp.int32, (own, LANES), 1)
    cut_left = [jnp.zeros((own, LANES), jnp.float32) for _ in range(groups)]
    for r in range(rows):
        for g in range(groups + 1):
            for side, slot in ((0, r), (1, rows + r)):
                target = g if side == 0 else g - 1
                if target < 0 or target >= groups:
                    continue
                value = jnp.zeros((own, LANES), jnp.float32)
                if g < groups:
                    value = pltpu.roll(packed[r, g, tiles[0][1]], slot, 1)
                if g > 0:
                    value = value - pltpu.roll(packed[r, g - 1, tiles[-1][1]], slot + 1, 1)
                cut_left[target] = jnp.where(lane == slot, value, cut_left[target])
    for g in range(groups):
        edge_send[g] = jnp.zeros((room, LANES), jnp.float32)
        edge_send[g, 0:own] = cut_left[g]
    for n in range(groups - 1):
        edge_copy(n).start()

    edges[my_edges, :] = edge_send[me]

    for load in loads[2:]:
        load.wait()
    first, second, term = triples[0:1, :], triples[1:2, :], triples[2:3, :]
    over = ratios[1:2, :]
    twelfths = jnp.where(over == 1, 12, jnp.where(over == 2, 6, jnp.where(over == 3, 4, 3)))
    amount = (ratios[0:1, :] * twelfths).astype(jnp.float32)
    at = lax.broadcasted_iota(jnp.int32, (8, total), 1)
    ids = jnp.broadcast_to(slots[...], (8, groups * own)).astype(jnp.float32)
    if total > groups * own:
        ids = jnp.concatenate([ids, jnp.zeros((8, total - groups * own), jnp.float32)], axis=1)
    spread = jnp.full((8, total), -2.0, jnp.float32)
    for s in range(groups):
        moved = pltpu.roll(ids, s * (room - own), 1) if s * (room - own) else ids
        spread = jnp.where((at >= s * room) & (at < s * room + own), moved, spread)
    mode = jnp.transpose(jnp.broadcast_to(spread[0:1, :], (total, total)))[:, 0:1].astype(jnp.int32)
    hit_first = jnp.where(mode == first, 1.0, 0.0).astype(jnp.bfloat16)
    hit_second = jnp.where(mode == second, amount, 0.0)
    for k in range(kl_terms):
        picked = jnp.where(term == k, hit_second, 0.0).astype(jnp.bfloat16)
        block = lax.dot_general(
            hit_first, picked, (((1,), (1,)), ((), ())), preferred_element_type=jnp.float32
        ).astype(jnp.bfloat16)
        weights[k * total : (k + 1) * total, 0:total] = block
        weights[k * total : (k + 1) * total, total : 2 * total] = block

    stage[...] = jnp.zeros((total, width), jnp.float32)

    def staged(part):
        for s in range(groups):
            for _, rows_of, cols_of in tiles:
                stage[s * room : s * room + own, cols_of] = part(s, rows_of)
        return stage[...]

    def store(target, value):
        for s in range(groups):
            for _, rows_of, cols_of in tiles:
                target[s, rows_of] = value[s * room : s * room + own, cols_of]

    def add(r, value):
        for s in range(groups):
            for _, rows_of, cols_of in tiles:
                done[r, s, rows_of] = done[r, s, rows_of] + value[s * room : s * room + own, cols_of]

    def flux(diff, coef):
        size = diff.shape[1]
        high = diff.astype(jnp.bfloat16)
        split[0:total, 0:size] = high
        split[total : 2 * total, 0:size] = (diff - high.astype(jnp.float32)).astype(jnp.bfloat16)
        mixed = jnp.dot(weights[...], split[:, 0:size], preferred_element_type=jnp.float32)
        result = coef[0:1, :] * mixed[0:total]
        for k in range(1, kl_terms):
            result = result + coef[k : k + 1, :] * mixed[k * total : (k + 1) * total]
        return result

    kl_lane = lax.broadcasted_iota(jnp.int32, (kl_terms, LANES), 1)
    before = pl.multiple_of(jnp.maximum(base - LANES, 0), LANES)
    after = pl.multiple_of(lax.rem(base + width, cols), LANES)
    not_first = jnp.where(me > 0, 1.0, 0.0)
    not_last = jnp.where(me < groups - 1, 1.0, 0.0)
    cut_coef = jnp.zeros((kl_terms, LANES), jnp.float32)
    for r in range(rows):
        here = pltpu.roll(klt[r, :, pl.ds(base, LANES)], r, 1) if r else klt[r, :, pl.ds(base, LANES)]
        there = pltpu.roll(klt[r, :, pl.ds(before, LANES)], r + 1, 1)
        cut_coef = jnp.where(kl_lane == r, (here + not_first * there) * SCALE, cut_coef)

    for n in range(groups - 1):
        edge_copy(n).wait_recv()
    total_lane = lax.broadcasted_iota(jnp.int32, (total, LANES), 1)
    cut_diff = edges[...]
    cut_flux = flux(jnp.where(total_lane < rows, cut_diff, 0.0), cut_coef)
    edge_send_flux = cut_flux

    wide_lane = lax.broadcasted_iota(jnp.int32, (total, width), 1)
    coef_lane = lax.broadcasted_iota(jnp.int32, (kl_terms, width), 1)

    def across(r):
        x = staged(lambda s, p: field[r + 1, s, p])
        right = jnp.sum(jnp.where(total_lane == rows + r, edges[...], 0.0), axis=1, keepdims=True)
        diff = jnp.where(wide_lane == width - 1, right, pltpu.roll(x, width - 1, 1) - x)
        a = klt[r, :, pl.ds(base, width)]
        a_next = klt[r, :, pl.ds(after, LANES)][:, 0:1] * not_last
        coef = (a + jnp.where(coef_lane == width - 1, a_next, pltpu.roll(a, width - 1, 1))) * SCALE
        flow = flux(diff, coef)
        left = jnp.sum(jnp.where(total_lane == r, edge_send_flux, 0.0), axis=1, keepdims=True)
        return jnp.where(wide_lane == 0, left, pltpu.roll(flow, 1, 1)) - flow

    wait_row(rows - 1)
    start_row(2)
    wait_row(0)
    start_row(3)

    @pl.when(has_prev)
    def _():
        rim_copy(1).start()

    @pl.when(has_next)
    def _():
        rim_copy(0).start()

    store(done.at[0], across(0))

    def one_row(r, carry):
        @pl.when(r < rows - 1)
        def _():
            wait_row(r)

        @pl.when(r + 3 < rows - 1)
        def _():
            start_row(r + 3)

        coef = (klt[r - 1, :, pl.ds(base, width)] + klt[r, :, pl.ds(base, width)]) * SCALE
        down = flux(staged(lambda s, p: field[r + 1, s, p] - field[r, s, p]), coef)
        add(r - 1, -down)

        @pl.when(r > 1)
        def _():
            send_row(r - 1)

        store(done.at[r], across(r) + down)
        return carry

    half = rows // 2
    lax.fori_loop(1, half, one_row, 0)

    @pl.when(has_prev)
    def _():
        rim_copy(0).wait_recv()
        kl_copy(0).wait_recv()

    @pl.when(jnp.logical_not(has_prev))
    def _():
        field[0] = jnp.zeros(field.shape[1:], jnp.float32)
        kl_rim[0] = jnp.zeros((kl_terms, width), jnp.float32)

    @pl.when(has_next)
    def _():
        rim_copy(1).wait_recv()
        kl_copy(1).wait_recv()

    @pl.when(jnp.logical_not(has_next))
    def _():
        field[rows + 1] = jnp.zeros(field.shape[1:], jnp.float32)
        kl_rim[1] = jnp.zeros((kl_terms, width), jnp.float32)

    coef = (kl_rim[0] + klt[0, :, pl.ds(base, width)]) * SCALE
    add(0, flux(staged(lambda s, p: field[1, s, p] - field[0, s, p]), coef))
    send_row(0)
    coef = (kl_rim[1] + klt[rows - 1, :, pl.ds(base, width)]) * SCALE
    last = flux(staged(lambda s, p: field[rows + 1, s, p] - field[rows, s, p]), coef)
    store(last_down, last)
    lax.fori_loop(half, rows, one_row, 0)
    done[rows - 1] = done[rows - 1] - last_down[...]
    send_row(rows - 1)

    order = list(range(1, half - 1)) + [0] + list(range(half - 1, rows))
    for r in order:
        back_copy(r).wait()
        for n in range(groups - 1):
            backward(r, n).wait_recv()
        for g in range(groups):
            for t, rows_of, _ in tiles:
                at = g * width + t * LANES
                out[:, r, at : at + LANES] = back[r, g, rows_of]

    def finish(r, carry):
        for n in range(groups - 1):
            forward(r, n).wait_send()
            backward(r, n).wait_send()
        return carry

    lax.fori_loop(0, rows, finish, 0)
    for n in range(groups - 1):
        edge_copy(n).wait_send()

    @pl.when(has_prev)
    def _():
        rim_copy(1).wait_send()
        kl_copy(1).wait_send()

    @pl.when(has_next)
    def _():
        rim_copy(0).wait_send()
        kl_copy(0).wait_send()


def local(modes, kl_fields, triples, ratios, mode_of_slot):
    groups, slabs = lax.axis_size("chaos"), lax.axis_size("space")
    own, rows, cols = modes.shape
    kl_terms = kl_fields.shape[0]
    padded = -(-own // 8) * 8
    total = groups * padded
    width = cols // groups
    slots = mode_of_slot.reshape(1, groups * own)
    table, amounts = triples.T, ratios.T
    block = (groups, own * (width // LANES), LANES)
    vmem, dma = pltpu.VMEM, pltpu.SemaphoreType.DMA
    result = pl.pallas_call(
        functools.partial(galerkin_kernel, groups, slabs),
        out_shape=jax.ShapeDtypeStruct((own, rows, cols), jnp.float32),
        in_specs=[pl.BlockSpec(memory_space=pltpu.HBM)] * 5,
        out_specs=pl.BlockSpec(memory_space=pltpu.VMEM),
        scratch_shapes=[
            vmem(modes.shape, jnp.float32),
            vmem(kl_fields.shape, jnp.float32),
            vmem(table.shape, jnp.int32),
            vmem(amounts.shape, jnp.int32),
            vmem(slots.shape, jnp.int32),
            vmem((rows,) + block, jnp.float32),
            vmem((rows, kl_terms, cols), jnp.float32),
            vmem((rows + 2,) + block, jnp.float32),
            vmem((total, LANES), jnp.float32),
            vmem((groups, padded, LANES), jnp.float32),
            vmem((2, kl_terms, width), jnp.float32),
            vmem((kl_terms * total, 2 * total), jnp.bfloat16),
            vmem((2 * total, width), jnp.bfloat16),
            vmem((rows,) + block, jnp.float32),
            vmem((rows,) + block, jnp.float32),
            vmem((total, width), jnp.float32),
            vmem(block, jnp.float32),
            dma((rows, groups - 1)), dma((rows, groups - 1)),
            dma((rows, groups - 1)), dma((rows, groups - 1)),
            dma((rows,)), dma((rows,)),
            dma((groups - 1,)), dma((groups - 1,)),
            dma((2,)), dma((2,)), dma((2,)), dma((2,)), dma((5,)),
        ],
        compiler_params=pltpu.CompilerParams(
            collective_id=0, has_side_effects=True, vmem_limit_bytes=60 * 1024 * 1024
        ),
    )(modes, kl_fields, table, amounts, slots)
    return result


def solution(mesh):
    return jax.shard_map(
        local,
        mesh=mesh,
        in_specs=(P("chaos", "space", None), P(None, "space", None), P(), P(), P()),
        out_specs=P("chaos", "space", None),
        check_vma=False,
    )
```

```python
import functools

import jax
import jax.numpy as jnp
from jax import lax
from jax.experimental import pallas as pl
from jax.experimental.pallas import tpu as pltpu
from jax.sharding import PartitionSpec as P

MESH = pl.DeviceIdType.MESH
LANES = 128
SCALE = 0.5 / 12.0


def galerkin_kernel(
    groups, slabs, modes_hbm, kl_hbm, triples_hbm, ratios_hbm, slots_hbm, out,
    modes, kl, triples, ratios, slots, packed, klt, field, edges, edge_send, kl_rim, weights, split, done, stage, last_down,
    fwd_send, fwd_recv, bwd_send, bwd_recv, own_sem, back_sem,
    edge_ssem, edge_rsem, rim_ssem, rim_rsem, kl_ssem, kl_rsem, load_sem,
):
    loads = [
        pltpu.make_async_copy(source, target, load_sem.at[n])
        for n, (source, target) in enumerate((
            (modes_hbm, modes), (kl_hbm, kl), (triples_hbm, triples),
            (ratios_hbm, ratios), (slots_hbm, slots),
        ))
    ]
    for load in loads:
        load.start()
    me = lax.axis_index("chaos")
    slab = lax.axis_index("space")
    own, rows, cols = modes.shape
    kl_terms = kl.shape[0]
    room = -(-own // 8) * 8
    total = groups * room
    width = cols // groups
    base = pl.multiple_of(me * width, LANES)
    tiles = [(t, slice(t * own, (t + 1) * own), slice(t * LANES, (t + 1) * LANES)) for t in range(width // LANES)]
    my_edges = pl.ds(pl.multiple_of(me * room, 8), room)
    has_prev = slab > 0
    has_next = slab < slabs - 1
    partners = [lax.rem(me + off, groups) for off in range(1, groups)]

    barrier = pltpu.get_barrier_semaphore()
    for peer in partners:
        pl.semaphore_signal(barrier, inc=1, device_id={"chaos": peer}, device_id_type=MESH)

    @pl.when(has_prev)
    def _():
        pl.semaphore_signal(barrier, inc=1, device_id={"space": slab - 1}, device_id_type=MESH)

    @pl.when(has_next)
    def _():
        pl.semaphore_signal(barrier, inc=1, device_id={"space": slab + 1}, device_id_type=MESH)

    ends = jnp.where(has_prev, 1, 0) + jnp.where(has_next, 1, 0)
    pl.semaphore_wait(barrier, groups - 1 + ends)

    def forward(r, n):
        peer = partners[n]
        return pltpu.make_async_remote_copy(
            src_ref=packed.at[r, peer],
            dst_ref=field.at[r + 1, me],
            send_sem=fwd_send.at[r, n], recv_sem=fwd_recv.at[r, n],
            device_id={"chaos": peer}, device_id_type=MESH,
        )

    def own_copy(r):
        return pltpu.make_async_copy(
            packed.at[r, me], field.at[r + 1, me], own_sem.at[r]
        )

    def backward(r, n):
        peer = partners[n]
        return pltpu.make_async_remote_copy(
            src_ref=done.at[r, peer],
            dst_ref=out.at[r, me],
            send_sem=bwd_send.at[r, n], recv_sem=bwd_recv.at[r, n],
            device_id={"chaos": peer}, device_id_type=MESH,
        )

    def back_copy(r):
        return pltpu.make_async_copy(
            done.at[r, me], out.at[r, me], back_sem.at[r]
        )

    def edge_copy(n):
        return pltpu.make_async_remote_copy(
            src_ref=edge_send.at[partners[n]], dst_ref=edges.at[my_edges],
            send_sem=edge_ssem.at[n], recv_sem=edge_rsem.at[n],
            device_id={"chaos": partners[n]}, device_id_type=MESH,
        )

    def rim_copy(up):
        return pltpu.make_async_remote_copy(
            src_ref=field.at[1 if up else rows], dst_ref=field.at[rows + 1 if up else 0],
            send_sem=rim_ssem.at[up], recv_sem=rim_rsem.at[up],
            device_id={"space": slab - 1 if up else slab + 1}, device_id_type=MESH,
        )

    def kl_copy(up):
        return pltpu.make_async_remote_copy(
            src_ref=klt.at[0 if up else rows - 1, :, pl.ds(base, width)],
            dst_ref=kl_rim.at[1 if up else 0],
            send_sem=kl_ssem.at[up], recv_sem=kl_rsem.at[up],
            device_id={"space": slab - 1 if up else slab + 1}, device_id_type=MESH,
        )

    def start_row(r):
        own_copy(r).start()
        for n in range(groups - 1):
            forward(r, n).start()

    def wait_row(r):
        own_copy(r).wait()
        for n in range(groups - 1):
            forward(r, n).wait_recv()

    def send_row(r):
        back_copy(r).start()
        for n in range(groups - 1):
            backward(r, n).start()

    loads[0].wait()
    for r in [rows - 1] + list(range(rows - 1)):
        for g in range(groups):
            for t, part, _ in tiles:
                at = g * width + t * LANES
                packed[r, g, part] = modes[:, r, at : at + LANES]
        if r in (rows - 1, 0, 1):
            start_row(r)
    loads[1].wait()
    for r in [0, rows - 1] + list(range(1, rows - 1)):
        klt[r] = kl[:, r, :]

    @pl.when(has_prev)
    def _():
        kl_copy(1).start()

    @pl.when(has_next)
    def _():
        kl_copy(0).start()

    lane = lax.broadcasted_iota(jnp.int32, (own, LANES), 1)
    cut_left = [jnp.zeros((own, LANES), jnp.float32) for _ in range(groups)]
    for r in range(rows):
        for g in range(groups + 1):
            for side, slot in ((0, r), (1, rows + r)):
                target = g if side == 0 else g - 1
                if target < 0 or target >= groups:
                    continue
                value = jnp.zeros((own, LANES), jnp.float32)
                if g < groups:
                    value = pltpu.roll(packed[r, g, tiles[0][1]], slot, 1)
                if g > 0:
                    value = value - pltpu.roll(packed[r, g - 1, tiles[-1][1]], slot + 1, 1)
                cut_left[target] = jnp.where(lane == slot, value, cut_left[target])
    for g in range(groups):
        edge_send[g] = jnp.zeros((room, LANES), jnp.float32)
        edge_send[g, 0:own] = cut_left[g]
    for n in range(groups - 1):
        edge_copy(n).start()

    edges[my_edges, :] = edge_send[me]
    start_row(2)

    for load in loads[2:]:
        load.wait()
    first, second, term = triples[0:1, :], triples[1:2, :], triples[2:3, :]
    over = ratios[1:2, :]
    twelfths = jnp.where(over == 1, 12, jnp.where(over == 2, 6, jnp.where(over == 3, 4, 3)))
    amount = (ratios[0:1, :] * twelfths).astype(jnp.float32)
    at = lax.broadcasted_iota(jnp.int32, (8, total), 1)
    ids = jnp.broadcast_to(slots[...], (8, groups * own)).astype(jnp.float32)
    if total > groups * own:
        ids = jnp.concatenate([ids, jnp.zeros((8, total - groups * own), jnp.float32)], axis=1)
    spread = jnp.full((8, total), -2.0, jnp.float32)
    for s in range(groups):
        moved = pltpu.roll(ids, s * (room - own), 1) if s * (room - own) else ids
        spread = jnp.where((at >= s * room) & (at < s * room + own), moved, spread)
    mode = jnp.transpose(jnp.broadcast_to(spread[0:1, :], (total, total)))[:, 0:1].astype(jnp.int32)
    hit_first = jnp.where(mode == first, 1.0, 0.0).astype(jnp.bfloat16)
    hit_second = jnp.where(mode == second, amount, 0.0)
    for k in range(kl_terms):
        picked = jnp.where(term == k, hit_second, 0.0).astype(jnp.bfloat16)
        block = lax.dot_general(
            hit_first, picked, (((1,), (1,)), ((), ())), preferred_element_type=jnp.float32
        ).astype(jnp.bfloat16)
        weights[k * total : (k + 1) * total, 0:total] = block
        weights[k * total : (k + 1) * total, total : 2 * total] = block

    stage[...] = jnp.zeros((total, width), jnp.float32)

    def staged(part):
        for s in range(groups):
            for _, rows_of, cols_of in tiles:
                stage[s * room : s * room + own, cols_of] = part(s, rows_of)
        return stage[...]

    def store(target, value):
        for s in range(groups):
            for _, rows_of, cols_of in tiles:
                target[s, rows_of] = value[s * room : s * room + own, cols_of]

    def add(r, value):
        for s in range(groups):
            for _, rows_of, cols_of in tiles:
                done[r, s, rows_of] = done[r, s, rows_of] + value[s * room : s * room + own, cols_of]

    def flux(diff, coef):
        size = diff.shape[1]
        high = diff.astype(jnp.bfloat16)
        split[0:total, 0:size] = high
        split[total : 2 * total, 0:size] = (diff - high.astype(jnp.float32)).astype(jnp.bfloat16)
        mixed = jnp.dot(weights[...], split[:, 0:size], preferred_element_type=jnp.float32)
        result = coef[0:1, :] * mixed[0:total]
        for k in range(1, kl_terms):
            result = result + coef[k : k + 1, :] * mixed[k * total : (k + 1) * total]
        return result

    kl_lane = lax.broadcasted_iota(jnp.int32, (kl_terms, LANES), 1)
    before = pl.multiple_of(jnp.maximum(base - LANES, 0), LANES)
    after = pl.multiple_of(lax.rem(base + width, cols), LANES)
    not_first = jnp.where(me > 0, 1.0, 0.0)
    not_last = jnp.where(me < groups - 1, 1.0, 0.0)
    cut_coef = jnp.zeros((kl_terms, LANES), jnp.float32)
    for r in range(rows):
        here = pltpu.roll(klt[r, :, pl.ds(base, LANES)], r, 1) if r else klt[r, :, pl.ds(base, LANES)]
        there = pltpu.roll(klt[r, :, pl.ds(before, LANES)], r + 1, 1)
        cut_coef = jnp.where(kl_lane == r, (here + not_first * there) * SCALE, cut_coef)

    for n in range(groups - 1):
        edge_copy(n).wait_recv()
    total_lane = lax.broadcasted_iota(jnp.int32, (total, LANES), 1)
    cut_diff = edges[...]
    cut_flux = flux(jnp.where(total_lane < rows, cut_diff, 0.0), cut_coef)
    edge_send_flux = cut_flux

    wide_lane = lax.broadcasted_iota(jnp.int32, (total, width), 1)
    coef_lane = lax.broadcasted_iota(jnp.int32, (kl_terms, width), 1)

    def across(r):
        x = staged(lambda s, p: field[r + 1, s, p])
        right = jnp.sum(jnp.where(total_lane == rows + r, edges[...], 0.0), axis=1, keepdims=True)
        diff = jnp.where(wide_lane == width - 1, right, pltpu.roll(x, width - 1, 1) - x)
        a = klt[r, :, pl.ds(base, width)]
        a_next = klt[r, :, pl.ds(after, LANES)][:, 0:1] * not_last
        coef = (a + jnp.where(coef_lane == width - 1, a_next, pltpu.roll(a, width - 1, 1))) * SCALE
        flow = flux(diff, coef)
        left = jnp.sum(jnp.where(total_lane == r, edge_send_flux, 0.0), axis=1, keepdims=True)
        return jnp.where(wide_lane == 0, left, pltpu.roll(flow, 1, 1)) - flow

    wait_row(rows - 1)
    start_row(3)
    wait_row(0)

    @pl.when(has_prev)
    def _():
        rim_copy(1).start()

    @pl.when(has_next)
    def _():
        rim_copy(0).start()

    store(done.at[0], across(0))

    def one_row(r, carry):
        wait_row(r)

        @pl.when(r + 3 < rows - 1)
        def _():
            start_row(r + 3)

        coef = (klt[r - 1, :, pl.ds(base, width)] + klt[r, :, pl.ds(base, width)]) * SCALE
        down = flux(staged(lambda s, p: field[r + 1, s, p] - field[r, s, p]), coef)
        add(r - 1, -down)

        @pl.when(r > 1)
        def _():
            send_row(r - 1)

        store(done.at[r], across(r) + down)
        return carry

    half = rows // 2
    lax.fori_loop(1, half, one_row, 0)

    @pl.when(has_prev)
    def _():
        rim_copy(0).wait_recv()
        kl_copy(0).wait_recv()

    @pl.when(jnp.logical_not(has_prev))
    def _():
        field[0] = jnp.zeros(field.shape[1:], jnp.float32)
        kl_rim[0] = jnp.zeros((kl_terms, width), jnp.float32)

    @pl.when(has_next)
    def _():
        rim_copy(1).wait_recv()
        kl_copy(1).wait_recv()

    @pl.when(jnp.logical_not(has_next))
    def _():
        field[rows + 1] = jnp.zeros(field.shape[1:], jnp.float32)
        kl_rim[1] = jnp.zeros((kl_terms, width), jnp.float32)

    coef = (kl_rim[0] + klt[0, :, pl.ds(base, width)]) * SCALE
    add(0, flux(staged(lambda s, p: field[1, s, p] - field[0, s, p]), coef))
    send_row(0)
    coef = (kl_rim[1] + klt[rows - 1, :, pl.ds(base, width)]) * SCALE
    last = flux(staged(lambda s, p: field[rows + 1, s, p] - field[rows, s, p]), coef)
    store(last_down, across(rows - 1) - last)
    lax.fori_loop(half, rows - 1, one_row, 0)
    coef = (klt[rows - 2, :, pl.ds(base, width)] + klt[rows - 1, :, pl.ds(base, width)]) * SCALE
    down = flux(staged(lambda s, p: field[rows, s, p] - field[rows - 1, s, p]), coef)
    add(rows - 2, -down)
    send_row(rows - 2)
    store(done.at[rows - 1], down)
    done[rows - 1] = done[rows - 1] + last_down[...]
    send_row(rows - 1)

    order = list(range(1, half - 1)) + [0] + list(range(half - 1, rows))
    for r in order:
        back_copy(r).wait()
        for n in range(groups - 1):
            backward(r, n).wait_recv()

    def finish(r, carry):
        for n in range(groups - 1):
            forward(r, n).wait_send()
            backward(r, n).wait_send()
        return carry

    lax.fori_loop(0, rows, finish, 0)
    for n in range(groups - 1):
        edge_copy(n).wait_send()

    @pl.when(has_prev)
    def _():
        rim_copy(1).wait_send()
        kl_copy(1).wait_send()

    @pl.when(has_next)
    def _():
        rim_copy(0).wait_send()
        kl_copy(0).wait_send()


def unpack_kernel(blocks, out):
    own, rows, width = out.shape
    for r in range(rows):
        for t in range(width // LANES):
            out[:, r, t * LANES : (t + 1) * LANES] = blocks[r, 0, t * own : (t + 1) * own]


def local(modes, kl_fields, triples, ratios, mode_of_slot):
    groups, slabs = lax.axis_size("chaos"), lax.axis_size("space")
    own, rows, cols = modes.shape
    kl_terms = kl_fields.shape[0]
    padded = -(-own // 8) * 8
    total = groups * padded
    width = cols // groups
    slots = mode_of_slot.reshape(1, groups * own)
    table, amounts = triples.T, ratios.T
    block = (groups, own * (width // LANES), LANES)
    vmem, dma = pltpu.VMEM, pltpu.SemaphoreType.DMA
    result = pl.pallas_call(
        functools.partial(galerkin_kernel, groups, slabs),
        out_shape=jax.ShapeDtypeStruct((rows,) + block, jnp.float32),
        in_specs=[pl.BlockSpec(memory_space=pltpu.HBM)] * 5,
        out_specs=pl.BlockSpec(memory_space=pltpu.HBM),
        scratch_shapes=[
            vmem(modes.shape, jnp.float32),
            vmem(kl_fields.shape, jnp.float32),
            vmem(table.shape, jnp.int32),
            vmem(amounts.shape, jnp.int32),
            vmem(slots.shape, jnp.int32),
            vmem((rows,) + block, jnp.float32),
            vmem((rows, kl_terms, cols), jnp.float32),
            vmem((rows + 2,) + block, jnp.float32),
            vmem((total, LANES), jnp.float32),
            vmem((groups, padded, LANES), jnp.float32),
            vmem((2, kl_terms, width), jnp.float32),
            vmem((kl_terms * total, 2 * total), jnp.bfloat16),
            vmem((2 * total, width), jnp.bfloat16),
            vmem((rows,) + block, jnp.float32),
            vmem((total, width), jnp.float32),
            vmem(block, jnp.float32),
            dma((rows, groups - 1)), dma((rows, groups - 1)),
            dma((rows, groups - 1)), dma((rows, groups - 1)),
            dma((rows,)), dma((rows,)),
            dma((groups - 1,)), dma((groups - 1,)),
            dma((2,)), dma((2,)), dma((2,)), dma((2,)), dma((5,)),
        ],
        compiler_params=pltpu.CompilerParams(
            collective_id=0, has_side_effects=True, vmem_limit_bytes=60 * 1024 * 1024
        ),
    )(modes, kl_fields, table, amounts, slots)
    return pl.pallas_call(
        unpack_kernel,
        grid=(groups,),
        out_shape=jax.ShapeDtypeStruct((own, rows, cols), jnp.float32),
        in_specs=[pl.BlockSpec((rows, 1) + block[1:], lambda g: (0, g, 0, 0))],
        out_specs=pl.BlockSpec((own, rows, width), lambda g: (0, 0, g)),
        compiler_params=pltpu.CompilerParams(vmem_limit_bytes=60 * 1024 * 1024),
    )(result)


def solution(mesh):
    return jax.shard_map(
        local,
        mesh=mesh,
        in_specs=(P("chaos", "space", None), P(None, "space", None), P(), P(), P()),
        out_specs=P("chaos", "space", None),
        check_vma=False,
    )
```

```python
import functools

import jax
import jax.numpy as jnp
from jax import lax
from jax.experimental import pallas as pl
from jax.experimental.pallas import tpu as pltpu
from jax.sharding import PartitionSpec as P

MESH = pl.DeviceIdType.MESH
LANES = 128
SCALE = 0.5 / 12.0


def galerkin_kernel(
    groups, slabs, modes_hbm, kl_hbm, triples_hbm, ratios_hbm, slots_hbm, out,
    modes, kl, triples, ratios, slots, packed, klt, field, edges, edge_send, kl_rim, weights, split, done, back, stage, last_down,
    fwd_send, fwd_recv, bwd_send, bwd_recv, own_sem, back_sem,
    edge_ssem, edge_rsem, rim_ssem, rim_rsem, kl_ssem, kl_rsem, load_sem,
):
    loads = [
        pltpu.make_async_copy(source, target, load_sem.at[n])
        for n, (source, target) in enumerate((
            (modes_hbm, modes), (kl_hbm, kl), (triples_hbm, triples),
            (ratios_hbm, ratios), (slots_hbm, slots),
        ))
    ]
    for load in loads:
        load.start()
    me = lax.axis_index("chaos")
    slab = lax.axis_index("space")
    own, rows, cols = modes.shape
    kl_terms = kl.shape[0]
    room = -(-own // 8) * 8
    total = groups * room
    width = cols // groups
    base = pl.multiple_of(me * width, LANES)
    tiles = [(t, slice(t * own, (t + 1) * own), slice(t * LANES, (t + 1) * LANES)) for t in range(width // LANES)]
    my_edges = pl.ds(pl.multiple_of(me * room, 8), room)
    has_prev = slab > 0
    has_next = slab < slabs - 1
    partners = [lax.rem(me + off, groups) for off in range(1, groups)]

    barrier = pltpu.get_barrier_semaphore()
    for peer in partners:
        pl.semaphore_signal(barrier, inc=1, device_id={"chaos": peer}, device_id_type=MESH)

    @pl.when(has_prev)
    def _():
        pl.semaphore_signal(barrier, inc=1, device_id={"space": slab - 1}, device_id_type=MESH)

    @pl.when(has_next)
    def _():
        pl.semaphore_signal(barrier, inc=1, device_id={"space": slab + 1}, device_id_type=MESH)

    ends = jnp.where(has_prev, 1, 0) + jnp.where(has_next, 1, 0)
    pl.semaphore_wait(barrier, groups - 1 + ends)

    def forward(r, n):
        peer = partners[n]
        return pltpu.make_async_remote_copy(
            src_ref=packed.at[r, peer],
            dst_ref=field.at[r + 1, me],
            send_sem=fwd_send.at[r, n], recv_sem=fwd_recv.at[r, n],
            device_id={"chaos": peer}, device_id_type=MESH,
        )

    def own_copy(r):
        return pltpu.make_async_copy(
            packed.at[r, me], field.at[r + 1, me], own_sem.at[r]
        )

    def backward(r, n):
        peer = partners[n]
        return pltpu.make_async_remote_copy(
            src_ref=done.at[r, peer],
            dst_ref=back.at[r, me],
            send_sem=bwd_send.at[r, n], recv_sem=bwd_recv.at[r, n],
            device_id={"chaos": peer}, device_id_type=MESH,
        )

    def back_copy(r):
        return pltpu.make_async_copy(
            done.at[r, me], back.at[r, me], back_sem.at[r]
        )

    def edge_copy(n):
        return pltpu.make_async_remote_copy(
            src_ref=edge_send.at[partners[n]], dst_ref=edges.at[my_edges],
            send_sem=edge_ssem.at[n], recv_sem=edge_rsem.at[n],
            device_id={"chaos": partners[n]}, device_id_type=MESH,
        )

    def rim_copy(up):
        return pltpu.make_async_remote_copy(
            src_ref=field.at[1 if up else rows], dst_ref=field.at[rows + 1 if up else 0],
            send_sem=rim_ssem.at[up], recv_sem=rim_rsem.at[up],
            device_id={"space": slab - 1 if up else slab + 1}, device_id_type=MESH,
        )

    def kl_copy(up):
        return pltpu.make_async_remote_copy(
            src_ref=klt.at[0 if up else rows - 1, :, pl.ds(base, width)],
            dst_ref=kl_rim.at[1 if up else 0],
            send_sem=kl_ssem.at[up], recv_sem=kl_rsem.at[up],
            device_id={"space": slab - 1 if up else slab + 1}, device_id_type=MESH,
        )

    def start_row(r):
        own_copy(r).start()
        for n in range(groups - 1):
            forward(r, n).start()

    def wait_row(r):
        own_copy(r).wait()
        for n in range(groups - 1):
            forward(r, n).wait_recv()

    def send_row(r):
        back_copy(r).start()
        for n in range(groups - 1):
            backward(r, n).start()

    loads[0].wait()
    for r in [rows - 1] + list(range(rows - 1)):
        for g in range(groups):
            for t, part, _ in tiles:
                at = g * width + t * LANES
                packed[r, g, part] = modes[:, r, at : at + LANES]
        if r in (rows - 1, 0, 1):
            start_row(r)
    loads[1].wait()
    for r in [0, rows - 1] + list(range(1, rows - 1)):
        klt[r] = kl[:, r, :]

    @pl.when(has_prev)
    def _():
        kl_copy(1).start()

    @pl.when(has_next)
    def _():
        kl_copy(0).start()

    lane = lax.broadcasted_iota(jnp.int32, (own, LANES), 1)
    cut_left = [jnp.zeros((own, LANES), jnp.float32) for _ in range(groups)]
    for r in range(rows):
        for g in range(groups + 1):
            for side, slot in ((0, r), (1, rows + r)):
                target = g if side == 0 else g - 1
                if target < 0 or target >= groups:
                    continue
                value = jnp.zeros((own, LANES), jnp.float32)
                if g < groups:
                    value = pltpu.roll(packed[r, g, tiles[0][1]], slot, 1)
                if g > 0:
                    value = value - pltpu.roll(packed[r, g - 1, tiles[-1][1]], slot + 1, 1)
                cut_left[target] = jnp.where(lane == slot, value, cut_left[target])
    for g in range(groups):
        edge_send[g] = jnp.zeros((room, LANES), jnp.float32)
        edge_send[g, 0:own] = cut_left[g]
    for n in range(groups - 1):
        edge_copy(n).start()

    edges[my_edges, :] = edge_send[me]
    start_row(2)

    for load in loads[2:]:
        load.wait()
    first, second, term = triples[0:1, :], triples[1:2, :], triples[2:3, :]
    over = ratios[1:2, :]
    twelfths = jnp.where(over == 1, 12, jnp.where(over == 2, 6, jnp.where(over == 3, 4, 3)))
    amount = (ratios[0:1, :] * twelfths).astype(jnp.float32)
    at = lax.broadcasted_iota(jnp.int32, (8, total), 1)
    ids = jnp.broadcast_to(slots[...], (8, groups * own)).astype(jnp.float32)
    if total > groups * own:
        ids = jnp.concatenate([ids, jnp.zeros((8, total - groups * own), jnp.float32)], axis=1)
    spread = jnp.full((8, total), -2.0, jnp.float32)
    for s in range(groups):
        moved = pltpu.roll(ids, s * (room - own), 1) if s * (room - own) else ids
        spread = jnp.where((at >= s * room) & (at < s * room + own), moved, spread)
    mode = jnp.transpose(jnp.broadcast_to(spread[0:1, :], (total, total)))[:, 0:1].astype(jnp.int32)
    hit_first = jnp.where(mode == first, 1.0, 0.0).astype(jnp.bfloat16)
    hit_second = jnp.where(mode == second, amount, 0.0)
    for k in range(kl_terms):
        picked = jnp.where(term == k, hit_second, 0.0).astype(jnp.bfloat16)
        block = lax.dot_general(
            hit_first, picked, (((1,), (1,)), ((), ())), preferred_element_type=jnp.float32
        ).astype(jnp.bfloat16)
        weights[k * total : (k + 1) * total, 0:total] = block
        weights[k * total : (k + 1) * total, total : 2 * total] = block

    stage[...] = jnp.zeros((total, width), jnp.float32)

    def staged(part):
        for s in range(groups):
            for _, rows_of, cols_of in tiles:
                stage[s * room : s * room + own, cols_of] = part(s, rows_of)
        return stage[...]

    def store(target, value):
        for s in range(groups):
            for _, rows_of, cols_of in tiles:
                target[s, rows_of] = value[s * room : s * room + own, cols_of]

    def add(r, value):
        for s in range(groups):
            for _, rows_of, cols_of in tiles:
                done[r, s, rows_of] = done[r, s, rows_of] + value[s * room : s * room + own, cols_of]

    def flux(diff, coef):
        size = diff.shape[1]
        high = diff.astype(jnp.bfloat16)
        split[0:total, 0:size] = high
        split[total : 2 * total, 0:size] = (diff - high.astype(jnp.float32)).astype(jnp.bfloat16)
        mixed = jnp.dot(weights[...], split[:, 0:size], preferred_element_type=jnp.float32)
        result = coef[0:1, :] * mixed[0:total]
        for k in range(1, kl_terms):
            result = result + coef[k : k + 1, :] * mixed[k * total : (k + 1) * total]
        return result

    kl_lane = lax.broadcasted_iota(jnp.int32, (kl_terms, LANES), 1)
    before = pl.multiple_of(jnp.maximum(base - LANES, 0), LANES)
    after = pl.multiple_of(lax.rem(base + width, cols), LANES)
    not_first = jnp.where(me > 0, 1.0, 0.0)
    not_last = jnp.where(me < groups - 1, 1.0, 0.0)
    cut_coef = jnp.zeros((kl_terms, LANES), jnp.float32)
    for r in range(rows):
        here = pltpu.roll(klt[r, :, pl.ds(base, LANES)], r, 1) if r else klt[r, :, pl.ds(base, LANES)]
        there = pltpu.roll(klt[r, :, pl.ds(before, LANES)], r + 1, 1)
        cut_coef = jnp.where(kl_lane == r, (here + not_first * there) * SCALE, cut_coef)

    for n in range(groups - 1):
        edge_copy(n).wait_recv()
    total_lane = lax.broadcasted_iota(jnp.int32, (total, LANES), 1)
    cut_diff = edges[...]
    cut_flux = flux(jnp.where(total_lane < rows, cut_diff, 0.0), cut_coef)
    edge_send_flux = cut_flux

    wide_lane = lax.broadcasted_iota(jnp.int32, (total, width), 1)
    coef_lane = lax.broadcasted_iota(jnp.int32, (kl_terms, width), 1)

    def across(r):
        x = staged(lambda s, p: field[r + 1, s, p])
        right = jnp.sum(jnp.where(total_lane == rows + r, edges[...], 0.0), axis=1, keepdims=True)
        diff = jnp.where(wide_lane == width - 1, right, pltpu.roll(x, width - 1, 1) - x)
        a = klt[r, :, pl.ds(base, width)]
        a_next = klt[r, :, pl.ds(after, LANES)][:, 0:1] * not_last
        coef = (a + jnp.where(coef_lane == width - 1, a_next, pltpu.roll(a, width - 1, 1))) * SCALE
        flow = flux(diff, coef)
        left = jnp.sum(jnp.where(total_lane == r, edge_send_flux, 0.0), axis=1, keepdims=True)
        return jnp.where(wide_lane == 0, left, pltpu.roll(flow, 1, 1)) - flow

    wait_row(rows - 1)
    start_row(3)
    wait_row(0)

    @pl.when(has_prev)
    def _():
        rim_copy(1).start()

    @pl.when(has_next)
    def _():
        rim_copy(0).start()

    store(done.at[0], across(0))

    def one_row(r, carry):
        wait_row(r)

        @pl.when(r + 3 < rows - 1)
        def _():
            start_row(r + 3)

        coef = (klt[r - 1, :, pl.ds(base, width)] + klt[r, :, pl.ds(base, width)]) * SCALE
        down = flux(staged(lambda s, p: field[r + 1, s, p] - field[r, s, p]), coef)
        add(r - 1, -down)

        @pl.when(r > 1)
        def _():
            send_row(r - 1)

        store(done.at[r], across(r) + down)
        return carry

    half = rows // 2
    lax.fori_loop(1, half, one_row, 0)

    @pl.when(has_prev)
    def _():
        rim_copy(0).wait_recv()
        kl_copy(0).wait_recv()

    @pl.when(jnp.logical_not(has_prev))
    def _():
        field[0] = jnp.zeros(field.shape[1:], jnp.float32)
        kl_rim[0] = jnp.zeros((kl_terms, width), jnp.float32)

    @pl.when(has_next)
    def _():
        rim_copy(1).wait_recv()
        kl_copy(1).wait_recv()

    @pl.when(jnp.logical_not(has_next))
    def _():
        field[rows + 1] = jnp.zeros(field.shape[1:], jnp.float32)
        kl_rim[1] = jnp.zeros((kl_terms, width), jnp.float32)

    coef = (kl_rim[0] + klt[0, :, pl.ds(base, width)]) * SCALE
    add(0, flux(staged(lambda s, p: field[1, s, p] - field[0, s, p]), coef))
    send_row(0)
    coef = (kl_rim[1] + klt[rows - 1, :, pl.ds(base, width)]) * SCALE
    last = flux(staged(lambda s, p: field[rows + 1, s, p] - field[rows, s, p]), coef)
    store(last_down, across(rows - 1) - last)
    lax.fori_loop(half, rows - 1, one_row, 0)
    coef = (klt[rows - 2, :, pl.ds(base, width)] + klt[rows - 1, :, pl.ds(base, width)]) * SCALE
    down = flux(staged(lambda s, p: field[rows, s, p] - field[rows - 1, s, p]), coef)
    add(rows - 2, -down)
    send_row(rows - 2)
    store(done.at[rows - 1], down)
    done[rows - 1] = done[rows - 1] + last_down[...]
    send_row(rows - 1)

    order = list(range(1, half - 1)) + [0] + list(range(half - 1, rows))
    for r in order:
        back_copy(r).wait()
        for n in range(groups - 1):
            backward(r, n).wait_recv()

        for g in range(groups):
            for t, rows_of, _ in tiles:
                at = g * width + t * LANES
                out[r, :, at : at + LANES] = back[r, g, rows_of]

    def finish(r, carry):
        for n in range(groups - 1):
            forward(r, n).wait_send()
            backward(r, n).wait_send()
        return carry

    lax.fori_loop(0, rows, finish, 0)
    for n in range(groups - 1):
        edge_copy(n).wait_send()

    @pl.when(has_prev)
    def _():
        rim_copy(1).wait_send()
        kl_copy(1).wait_send()

    @pl.when(has_next)
    def _():
        rim_copy(0).wait_send()
        kl_copy(0).wait_send()


def local(modes, kl_fields, triples, ratios, mode_of_slot):
    groups, slabs = lax.axis_size("chaos"), lax.axis_size("space")
    own, rows, cols = modes.shape
    kl_terms = kl_fields.shape[0]
    padded = -(-own // 8) * 8
    total = groups * padded
    width = cols // groups
    slots = mode_of_slot.reshape(1, groups * own)
    table, amounts = triples.T, ratios.T
    block = (groups, own * (width // LANES), LANES)
    vmem, dma = pltpu.VMEM, pltpu.SemaphoreType.DMA
    result = pl.pallas_call(
        functools.partial(galerkin_kernel, groups, slabs),
        out_shape=jax.ShapeDtypeStruct((rows, own, cols), jnp.float32),
        in_specs=[pl.BlockSpec(memory_space=pltpu.HBM)] * 5,
        out_specs=pl.BlockSpec(memory_space=pltpu.VMEM),
        scratch_shapes=[
            vmem(modes.shape, jnp.float32),
            vmem(kl_fields.shape, jnp.float32),
            vmem(table.shape, jnp.int32),
            vmem(amounts.shape, jnp.int32),
            vmem(slots.shape, jnp.int32),
            vmem((rows,) + block, jnp.float32),
            vmem((rows, kl_terms, cols), jnp.float32),
            vmem((rows + 2,) + block, jnp.float32),
            vmem((total, LANES), jnp.float32),
            vmem((groups, padded, LANES), jnp.float32),
            vmem((2, kl_terms, width), jnp.float32),
            vmem((kl_terms * total, 2 * total), jnp.bfloat16),
            vmem((2 * total, width), jnp.bfloat16),
            vmem((rows,) + block, jnp.float32),
            vmem((rows,) + block, jnp.float32),
            vmem((total, width), jnp.float32),
            vmem(block, jnp.float32),
            dma((rows, groups - 1)), dma((rows, groups - 1)),
            dma((rows, groups - 1)), dma((rows, groups - 1)),
            dma((rows,)), dma((rows,)),
            dma((groups - 1,)), dma((groups - 1,)),
            dma((2,)), dma((2,)), dma((2,)), dma((2,)), dma((5,)),
        ],
        compiler_params=pltpu.CompilerParams(
            collective_id=0, has_side_effects=True, vmem_limit_bytes=60 * 1024 * 1024
        ),
    )(modes, kl_fields, table, amounts, slots)
    return jnp.transpose(result, (1, 0, 2))


def solution(mesh):
    return jax.shard_map(
        local,
        mesh=mesh,
        in_specs=(P("chaos", "space", None), P(None, "space", None), P(), P(), P()),
        out_specs=P("chaos", "space", None),
        check_vma=False,
    )
```
